128 devices in a mesh: band: 4 (over x), set: 32 (over y, z, core).
Axes of the slice: x: 4, y: 4, z: 4, core: 2. Of those that a mesh axis runs over, the one named last changes fastest.
Arguments:
- fields: bfloat16 [2560, 16, 5120], P(('band', 'set')), may hold values from -6 to 6
- depart: int32 [2560, 40, 4], P(('band', 'set')), may hold values from 0 to 102399, as said below
- blend: float32 [2560, 40, 4, 128], P(('band', 'set')), may hold values from 0.05 to 0.45
- wave_owner: int32 [1280], replicated, may hold values from 0 to 1279, each once
- damping: float32 [16], replicated, may hold values from 0.5 to 8
Outputs:
- updated: bfloat16 [2560, 16, 5120], P(('band', 'set'))
- spectra: float32 [1280, 16, 2, 1280], P(('band', 'set'))
The draws below stay inside these ranges and needn't reach their ends.
Inputs may be any that keep to these rules, and one draw needn't show every extreme that they name: The cycle depart[r, b, k] // 40 lies within 4 cycles of r; on every device some entry lies exactly 4 cycles away. `wave_owner`: each zonal wavenumber appears exactly once.
All inputs are finite; a program needn't handle non-finite values.
Results may differ from the reference program's by a relative error of at most 0.0077.
Values may be sent and summed in bfloat16 or wider, within the bound.
A program may use at most 192 MiB of HBM per device.

```python
import math
import jax
import jax.numpy as jnp
from jax import lax

NLAT = 2560
NLON = 5120
MM = 1280
LEV = 8
BW = 128
K = 4
HALO = 4
FL = 16
NB = 40


def draw_depart(key, part):
    key = jax.random.fold_in(key, 7)
    key_off, key_sign, key_lon = jax.random.split(key, 3)
    cycles = jnp.arange(NLAT, dtype=jnp.int32)[:, None, None]
    offsets = jax.random.randint(key_off, (NLAT, NB, K), -HALO, HALO + 1)
    signs = 2 * jax.random.randint(key_sign, (NLAT, NB, 1), 0, 2) - 1
    slot_ids = jnp.arange(K, dtype=jnp.int32)[None, None, :]
    offsets = jnp.where(slot_ids == K - 1, signs * HALO, offsets)
    src_cycle = jnp.clip(cycles + offsets, 0, NLAT - 1)
    lon_blocks = jnp.arange(NB, dtype=jnp.int32)[None, :, None]
    lon_shift = jax.random.randint(key_lon, (NLAT, NB, K), -2, 3)
    src_block = (lon_blocks + lon_shift) % NB
    return (src_cycle * NB + src_block).astype(jnp.int32)


def block_levels(own_key, dims, pieces, low, high):
    gain = 1.0
    for dim, shards_of in pieces:
        heights = jax.random.uniform(jax.random.fold_in(jax.random.fold_in(own_key, 6), dim), (shards_of,), jnp.float32, low / len(pieces), high / len(pieces))
        gain = gain * jnp.repeat(jnp.exp(heights), dims[dim] // shards_of).reshape((-1,) + (1,) * (len(dims) - 1 - dim))
    return gain


def gaussian(stream_key, extent, scale, most, pieces=(), kind=jnp.bfloat16):
    values = scale * jax.random.normal(stream_key, extent, jnp.float32)
    if pieces:
        values = values * block_levels(stream_key, extent, pieces, -0.22, 0.18)
    return jnp.clip(values, -most, most).astype(kind)


def setup_inputs(seed: int = 0) -> dict:
    key_of = jax.random.split(jax.random.key(seed), 6)
    fields = gaussian(key_of[0], (NLAT, FL, NLON), 1.0, 6.0, ((0, 128),))
    depart = draw_depart(jax.random.fold_in(key_of[5], 71), 0)
    blend = jnp.clip(0.05 + 0.39999999 * jax.random.uniform(key_of[2], (NLAT, NB, K, BW), jnp.float32) ** block_levels(key_of[2], (NLAT, NB, K, BW), ((0, 128),), -0.2, 0.2), 0.05, 0.45)
    wave_owner = jax.random.permutation(key_of[3], MM).astype(jnp.int32)
    damping = jnp.clip(jnp.exp(jax.random.uniform(key_of[4], (FL,), jnp.float32, math.log(0.5), math.log(8.0))), 0.5, 8.0)
    return dict(fields=fields, depart=depart, blend=blend, wave_owner=wave_owner, damping=damping)


def forward_table(columns, wavenums):
    index_mod = columns[:, None] * wavenums[None, :] % NLON
    angles = index_mod.astype(jnp.float32) * (2.0 * math.pi / NLON)
    norm_scale = math.sqrt(2.0 / NLON)
    stacked = jnp.stack([norm_scale * jnp.cos(angles), -norm_scale * jnp.sin(angles)], axis=1)
    return stacked.reshape(columns.shape[0], 2 * wavenums.shape[0]).astype(jnp.bfloat16)

def backward_table(columns, wavenums):
    index_mod = wavenums[:, None] * columns[None, :] % NLON
    angles = index_mod.astype(jnp.float32) * (2.0 * math.pi / NLON)
    weight = jnp.where(wavenums == 0, 0.5, 1.0).astype(jnp.float32) * math.sqrt(2.0 / NLON)
    stacked = jnp.stack([weight[:, None] * jnp.cos(angles), -weight[:, None] * jnp.sin(angles)], axis=0)
    return stacked.reshape(2 * wavenums.shape[0], columns.shape[0]).astype(jnp.bfloat16)

def basis_rows(first, count):
    orders = first + jnp.arange(count, dtype=jnp.int32)
    lat_index = jnp.arange(NLAT, dtype=jnp.int32)
    index_mod = orders[:, None] * (2 * lat_index[None, :] + 1) % (4 * NLAT)
    angles = index_mod.astype(jnp.float32) * (math.pi / (2 * NLAT))
    norm_scale = jnp.where(orders == 0, math.sqrt(1.0 / NLAT), math.sqrt(2.0 / NLAT)).astype(jnp.float32)
    return norm_scale[:, None] * jnp.cos(angles)

def damping_factors(damping):
    orders = jnp.arange(MM, dtype=jnp.int32).astype(jnp.float32)
    ratio = orders * (orders + 1.0) / (MM * (MM - 1.0))
    level_ids = jnp.arange(damping.shape[0], dtype=jnp.int32)
    powered = jnp.where(level_ids[:, None] < LEV, ratio[None, :] * ratio[None, :], ratio[None, :])
    return 1.0 / (1.0 + damping[:, None] * powered)

def reference(fields, depart, blend, wave_owner, damping):
    grid_view = fields.reshape(NLAT, FL, NB, BW)
    src_cycle = depart // NB
    src_block = depart % NB
    summed = jnp.zeros((NLAT, NB, FL, BW), jnp.float32)
    for k in range(K):
        gathered = grid_view[src_cycle[:, :, k], :, src_block[:, :, k], :]
        summed = summed + blend[:, :, k, None, :] * gathered.astype(jnp.float32)
    departed = summed.transpose(0, 2, 1, 3).reshape(NLAT, FL, NLON).astype(jnp.bfloat16)
    columns = jnp.arange(NLON, dtype=jnp.int32)
    coeffs = jnp.dot(departed.reshape(NLAT * FL, NLON), forward_table(columns, wave_owner), preferred_element_type=jnp.float32)
    fourier = coeffs.astype(jnp.bfloat16).reshape(NLAT, FL, 2, MM)
    basis = basis_rows(0, MM)
    spectra = jnp.einsum('jfck,nj->kfcn', fourier.astype(jnp.float32), basis, precision=lax.Precision.HIGHEST)
    orders = jnp.arange(MM, dtype=jnp.int32)
    keep_mask = (orders[None, :] >= wave_owner[:, None]).astype(jnp.float32)
    spectra = spectra * damping_factors(damping)[None, :, None, :] * keep_mask[:, None, None, :]
    zonal = jnp.einsum('kfcn,nj->jfck', spectra, basis, precision=lax.Precision.HIGHEST).astype(jnp.bfloat16)
    result = jnp.dot(zonal.reshape(NLAT * FL, 2 * MM), backward_table(columns, wave_owner), preferred_element_type=jnp.float32)
    updated = result.astype(jnp.bfloat16).reshape(NLAT, FL, NLON)
    return (updated, spectra)
```

```python
import functools
import math

import jax
import jax.numpy as jnp
import ml_dtypes
import numpy as np
from jax import lax
from jax.experimental import pallas as pl
from jax.experimental.pallas import tpu as pltpu
from jax.sharding import PartitionSpec as P

NLAT = 2560
NLON = 5120
MM = 1280
LEV = 8
BW = 128
K = 4
HALO = 4
FL = 16
NB = 40
ROWS = 20
NDEV = 128
OWN = 10
TQ = 5
NG = 10
COLS = 384
MESH = pl.DeviceIdType.MESH
BF = jnp.bfloat16
F32 = jnp.float32


def group_waves(g):
    m2 = np.arange(64)
    if g == 0:
        return 20 * m2, 10 + 20 * m2
    return g + 20 * m2, 20 - g + 20 * m2


@functools.lru_cache(None)
def forward_tables():
    s = math.sqrt(2.0 / NLON)
    i = np.arange(256)
    out = np.zeros((NG, 512, 256))
    for g in range(NG):
        lo, hi = group_waves(g)
        for half, m in ((0, lo), (1, hi)):
            a = 2 * np.pi * ((i[:, None] * m[None, :]) % NLON) / NLON
            c, sn = s * np.cos(a), s * np.sin(a)
            re = slice(64 * half, 64 * half + 64)
            im = slice(128 + 64 * half, 192 + 64 * half)
            if g == 0:
                rows = slice(256 * half, 256 * half + 256)
                out[g, rows, re] = c
                out[g, rows, im] = -sn
            else:
                sign = 1.0 if half == 0 else -1.0
                out[g, :256, re] = c
                out[g, :256, im] = -sn
                out[g, 256:, re] = sign * sn
                out[g, 256:, im] = sign * c
    return out.astype(ml_dtypes.bfloat16)


@functools.lru_cache(None)
def inverse_tables():
    s = math.sqrt(2.0 / NLON)
    i = np.arange(256)
    out = np.zeros((NG, 256, 512))
    for g in range(NG):
        lo, hi = group_waves(g)
        for half, m in ((0, lo), (1, hi)):
            a = 2 * np.pi * ((m[:, None] * i[None, :]) % NLON) / NLON
            w = np.where(m == 0, 0.5, 1.0)[:, None] * s
            c, sn = w * np.cos(a), w * np.sin(a)
            re = slice(64 * half, 64 * half + 64)
            im = slice(128 + 64 * half, 192 + 64 * half)
            if g == 0:
                cols = slice(256 * half, 256 * half + 256)
                out[g, re, cols] = c
                out[g, im, cols] = -sn
            else:
                sign = 1.0 if half == 0 else -1.0
                out[g, re, :256] = c
                out[g, im, :256] = -sn
                out[g, re, 256:] = sign * sn
                out[g, im, 256:] = sign * c
    return out.astype(ml_dtypes.bfloat16)


@functools.lru_cache(None)
def latitude_tables():
    t, r, sl = np.meshgrid(np.arange(TQ), np.arange(4), np.arange(64), indexing="ij")
    j = (20 * sl + 4 * t + r).reshape(-1)
    n = np.arange(MM)
    g = np.where(n == 0, math.sqrt(1.0 / NLAT), math.sqrt(2.0 / NLAT))
    b = g[:, None] * np.cos(np.pi * ((n[:, None] * (2 * j[None, :] + 1)) % (4 * NLAT)) / (2 * NLAT))
    be, bo = b[0::2], b[1::2]
    fwd = np.stack([be, bo]).astype(ml_dtypes.bfloat16)
    bwd = np.stack([be.T, bo.T]).astype(ml_dtypes.bfloat16)
    return np.ascontiguousarray(fwd), np.ascontiguousarray(bwd)


C1, C2 = math.cos(2 * math.pi / 5), math.cos(4 * math.pi / 5)
S1, S2 = math.sin(2 * math.pi / 5), math.sin(4 * math.pi / 5)


def five_parts(x):
    e1, e2 = x[1] + x[4], x[2] + x[3]
    o1, o2 = x[1] - x[4], x[2] - x[3]
    total = x[0] + (e1 + e2)
    return total, x[0] + C1 * e1 + C2 * e2, x[0] + C2 * e1 + C1 * e2, S1 * o1 + S2 * o2, S2 * o1 - S1 * o2


def dft20(d):
    alpha, beta, gr, gi = [], [], [], []
    for q in range(5):
        v = [None] * 4
        for b in (q, q + 5, q + 10, q + 15):
            v[b % 4] = d[b]
        e, o = v[0] + v[2], v[1] + v[3]
        alpha.append(e + o)
        beta.append(e - o)
        gr.append(v[0] - v[2])
        gi.append(v[3] - v[1])
    out = [None] * 11
    s, e1, e2, o1, o2 = five_parts(alpha)
    out[0], out[4], out[8] = (s, None), (e1, -o1), (e2, -o2)
    s, e1, e2, o1, o2 = five_parts(beta)
    out[10], out[6], out[2] = (s, None), (e1, o1), (e2, o2)
    s, e1, e2, o1, o2 = five_parts(gr)
    t, f1, f2, p1, p2 = five_parts(gi)
    out[5] = (s, t)
    out[9] = (e1 + p1, f1 - o1)
    out[1] = (e1 - p1, f1 + o1)
    out[7] = (e2 + p2, o2 - f2)
    out[3] = (e2 - p2, -(f2 + o2))
    return out


def idft20(c):
    a, bb, dr, di = [], [], [], []

    def spread(x0, pr, mi):
        ev1 = x0 + C1 * pr[0] + C2 * pr[1]
        ev2 = x0 + C2 * pr[0] + C1 * pr[1]
        od1 = S1 * mi[0] + S2 * mi[1]
        od2 = S2 * mi[0] - S1 * mi[1]
        return [x0 + (pr[0] + pr[1]), ev1 + od1, ev2 + od2, ev2 - od2, ev1 - od1]

    a = spread(c[0][0], (c[4][0], c[8][0]), (-c[4][1], -c[8][1]))
    bb = spread(c[10][0], (c[6][0], c[2][0]), (c[6][1], c[2][1]))
    dr = spread(
        c[5][0],
        (c[1][0] + c[9][0], c[3][0] + c[7][0]),
        (c[1][1] - c[9][1], c[7][1] - c[3][1]),
    )
    di = spread(
        c[5][1],
        (c[1][1] + c[9][1], -(c[3][1] + c[7][1])),
        (c[9][0] - c[1][0], c[7][0] - c[3][0]),
    )
    plus = [a[q] + bb[q] for q in range(5)]
    minus = [a[q] - bb[q] for q in range(5)]
    out = []
    for b in range(20):
        q = b % 5
        base = plus[q] if b % 2 == 0 else minus[q]
        r = b % 4
        out.append(base + dr[q] if r == 0 else base - di[q] if r == 1 else base - dr[q] if r == 2 else base + di[q])
    return out


def my_index():
    return lax.axis_index("band") * 32 + lax.axis_index("set")


def local_row(me, p):
    return jnp.where(me < NDEV // 2, p, ROWS - 1 - p)


def slot_of(d):
    return jnp.where(d < NDEV // 2, d, 3 * NDEV // 2 - 1 - d)


def one_hot(nat_ref, out_ref):
    def chunk(i, c):
        rows = pl.ds(pl.multiple_of(i * 128, 128), 128)
        lanes = lax.broadcasted_iota(jnp.int32, (128, MM), 1)
        out_ref[rows, :] = jnp.where(nat_ref[rows, :] == lanes, 1.0, 0.0).astype(BF)
        return c

    lax.fori_loop(0, NB // 4, chunk, 0)


def grid_kernel(lo_ref, mid_ref, hi_ref, dep_ref, blend_ref, nat_ref, tab_ref, out_ref,
                src, dep_f, g_buf, f_buf, hot, sem):
    me = my_index()
    copies = []
    for part, (ref, first, count) in enumerate(((lo_ref, 0, HALO), (mid_ref, HALO, ROWS), (hi_ref, HALO + ROWS, HALO))):
        for b in range(NB):
            copies.append(pltpu.make_async_copy(
                ref.at[:, :, pl.ds(b * BW, BW)], src.at[pl.ds(first, count), b], sem.at[part * NB + b]))
    for c in copies:
        c.start()
    one_hot(nat_ref, hot)
    for c in copies:
        c.wait()
    base = (me * ROWS - HALO) * NB

    def cycle(p, carry):
        r = local_row(me, p)
        for b in range(NB):
            total = None
            for k in range(K):
                at = dep_ref[(r * NB + b) * K + k] - base
                cyc = at // NB
                tile = src[cyc, at - cyc * NB].astype(F32)
                term = blend_ref[r, b, pl.ds(k, 1), :] * tile
                total = term if total is None else total + term
            dep_f[b // 2, :, pl.ds((b % 2) * BW, BW)] = total
        rows = pl.ds(pl.multiple_of(p * FL, FL), FL)
        for half in range(2):
            lanes = pl.ds(half * 128, 128)
            g = dft20([dep_f[b, :, lanes] for b in range(20)])
            pairs = [(g[0][0], g[10][0])] + [g[i] for i in range(1, 10)]
            for i, (re, im) in enumerate(pairs):
                g_buf[i, rows, pl.ds(half * 128, 128)] = re.astype(BF)
                g_buf[i, rows, pl.ds(256 + half * 128, 128)] = im.astype(BF)
        return carry

    lax.fori_loop(0, ROWS, cycle, 0)

    def group(g, carry):
        v = jnp.dot(g_buf[g], tab_ref[g], preferred_element_type=F32).astype(BF)
        lanes = pl.ds(pl.multiple_of(g * 128, 128), 128)
        f_buf[:, 0, :, lanes] = v[:, :128].reshape(ROWS, FL, 128)
        f_buf[:, 1, :, lanes] = v[:, 128:].reshape(ROWS, FL, 128)
        return carry

    lax.fori_loop(0, NG, group, 0)

    def order(i, carry):
        rows = pl.ds(pl.multiple_of(i * 256, 256), 256)
        v = lax.dot_general(hot[rows, :], f_buf[...].reshape(ROWS * 32, MM), (((1,), (1,)), ((), ())),
                            preferred_element_type=F32).astype(BF)
        for t in range(TQ):
            out_ref[t, rows, :] = v[:, t * 128:(t + 1) * 128]
        return carry

    lax.fori_loop(0, MM // 256, order, 0)


def block_swap(x):
    lane = lax.broadcasted_iota(jnp.int32, x[0].shape, 1)
    low64 = lane < 64
    low32 = (lane % 64) < 32
    z = [None] * 4
    for a in range(2):
        lo, hi = x[a], x[a + 2]
        z[a] = jnp.where(low64, lo, pltpu.roll(hi, 64, 1))
        z[a + 2] = jnp.where(low64, pltpu.roll(lo, 64, 1), hi)
    y = [None] * 4
    for a in (0, 2):
        lo, hi = z[a], z[a + 1]
        y[a] = jnp.where(low32, lo, pltpu.roll(hi, 32, 1))
        y[a + 1] = jnp.where(low32, pltpu.roll(lo, 96, 1), hi)
    return y


def lat_kernel(x_ref, fwd_ref, bwd_ref, damp_ref, wave_ref, spec_ref, out_ref, xf, uv, sbuf, s16, zf):
    def widen(i, c):
        rows = pl.ds(pl.multiple_of(i * 256, 256), 256)
        xf[rows, :] = x_ref[rows, :].astype(F32)
        return c

    lax.fori_loop(0, 25, widen, 0)

    def fold(i, carry):
        t, sc = i // 4, i % 4
        for g in range(3):
            us, vs = [], []
            for m in range(4 * g, 4 * g + 4):
                if m >= OWN:
                    us.append(jnp.zeros((16, 128), F32))
                    vs.append(jnp.zeros((16, 128), F32))
                    continue
                lo = xf[pl.ds(sc * 16 * 50 + t * OWN + m, 16, stride=50), :]
                hi = xf[pl.ds((64 + sc * 16) * 50 + t * OWN + m, 16, stride=50), :]
                us.append(lo + hi)
                vs.append(lo - hi)
            for par, vals in ((0, us), (1, vs)):
                y = block_swap(vals)
                for r in range(4):
                    rows = pl.ds(pl.multiple_of((t * 4 + r) * 64 + sc * 16, 16), 16)
                    uv[par, rows, pl.ds(g * 128, 128)] = y[r].astype(BF)
        return carry

    lax.fori_loop(0, 20, fold, 0)

    lane = lax.broadcasted_iota(jnp.int32, (1, COLS), 1)
    squared = (lane % FL) < LEV

    def analyse(i, carry):
        rows = pl.ds(pl.multiple_of(i * 128, 128), 128)
        for par in range(2):
            v = jnp.dot(fwd_ref[par, rows, :], uv[par], preferred_element_type=F32)
            n = 2 * (i * 128 + lax.broadcasted_iota(jnp.int32, (128, COLS), 0)) + par
            nf = n.astype(F32)
            q = nf * (nf + 1.0) * (1.0 / (MM * (MM - 1.0)))
            qp = jnp.where(squared, q * q, q)
            v = v * (1.0 / (1.0 + damp_ref[...] * qp))
            v = jnp.where(n >= wave_ref[...], v, 0.0)
            sbuf[pl.ds(i * 256 + par, 128, stride=2), :] = v[:, :128]
            sbuf[pl.ds(MM + i * 256 + par, 128, stride=2), :] = v[:, 128:256]
            sbuf[pl.ds(2 * MM + i * 256 + par, 128, stride=2), :] = v[:, 256:]
            s16[par, rows, :] = v.astype(BF)
        return carry

    lax.fori_loop(0, 5, analyse, 0)

    def synth(t, carry):
        rows = pl.ds(pl.multiple_of(t * 256, 256), 256)
        p = jnp.dot(bwd_ref[0, rows, :], s16[0], preferred_element_type=F32)
        q = jnp.dot(bwd_ref[1, rows, :], s16[1], preferred_element_type=F32)
        for half, z in ((0, p + q), (1, p - q)):
            for g in range(3):
                y = block_swap([z[r * 64:(r + 1) * 64, g * 128:(g + 1) * 128] for r in range(4)])
                for m in range(4 * g, min(4 * g + 4, OWN)):
                    zf[pl.ds(half * 64 * 50 + t * OWN + m, 64, stride=50), :] = y[m - 4 * g]
        return carry

    lax.fori_loop(0, TQ, synth, 0)

    def narrow(i, c):
        rows = pl.ds(pl.multiple_of(i * 256, 256), 256)
        out_ref[rows, :] = zf[rows, :].astype(BF)
        return c

    lax.fori_loop(0, 25, narrow, 0)

    for g in range(3):
        for nt in range(10):
            tr = jnp.transpose(sbuf[pl.ds(g * MM + nt * 128, 128), :])
            for m in range(4 * g, min(4 * g + 4, OWN)):
                for c in range(2):
                    first = (m - 4 * g) * 32 + c * 16
                    spec_ref[m, :, c, pl.ds(nt * 128, 128)] = tr[first:first + 16]


def wave_kernel(x_ref, nat_ref, tab_ref, out_ref, zt, hot, zn, h_buf):
    me = my_index()
    one_hot(nat_ref, hot)

    def turn(t, carry):
        zt[pl.ds(pl.multiple_of(t * 128, 128), 128), :] = jnp.transpose(x_ref[t])
        return carry

    lax.fori_loop(0, TQ, turn, 0)

    def order(i, carry):
        lanes = pl.ds(pl.multiple_of(i * 256, 256), 256)
        v = jnp.dot(zt[...], hot[:, lanes], preferred_element_type=F32).astype(BF)
        zn[:, :, :, lanes] = v.reshape(ROWS, 2, FL, 256)
        return carry

    lax.fori_loop(0, MM // 256, order, 0)

    def group(g, carry):
        lanes = pl.ds(pl.multiple_of(g * 128, 128), 128)
        re = zn[:, 0, :, lanes].reshape(ROWS * FL, 128)
        im = zn[:, 1, :, lanes].reshape(ROWS * FL, 128)
        v = jnp.concatenate([re, im], axis=1)
        h_buf[g] = jnp.dot(v, tab_ref[g], preferred_element_type=F32)
        return carry

    lax.fori_loop(0, NG, group, 0)

    def cycle(p, carry):
        r = local_row(me, p)
        rows = pl.ds(pl.multiple_of(p * FL, FL), FL)
        for half in range(2):
            re = [h_buf[g, rows, pl.ds(half * 128, 128)] for g in range(NG)]
            im = [h_buf[g, rows, pl.ds(256 + half * 128, 128)] for g in range(NG)]
            c = [(re[0], None)] + [(re[g], im[g]) for g in range(1, NG)] + [(im[0], None)]
            y = idft20(c)
            for b in range(20):
                out_ref[r, :, pl.ds(b * 256 + half * 128, 128)] = y[b].astype(BF)
        return carry

    lax.fori_loop(0, ROWS, cycle, 0)


def partner(i):
    x = lax.axis_index("band")
    st = lax.axis_index("set")
    j = lax.rem(i * 37, NDEV)
    tx = lax.rem(x + j // 32, 4)
    ty = lax.rem(st // 8 + lax.rem(j // 8, 4), 4)
    tz = lax.rem(lax.rem(st // 2, 4) + lax.rem(j // 2, 4), 4)
    tc = lax.rem(lax.rem(st, 2) + lax.rem(j, 2), 2)
    return tx, (ty * 4 + tz) * 2 + tc


def exchange_kernel(to_owner, x_ref, o_ref, ssem, rsem, lsem):
    me = my_index()

    def ends(d):
        if to_owner:
            return x_ref.at[:, pl.ds(d * 5, 5)], o_ref.at[slot_of(me)]
        return x_ref.at[slot_of(d)], o_ref.at[:, pl.ds(me * 5, 5)]

    own = pltpu.make_async_copy(*ends(me), lsem)
    own.start()

    def copy(i):
        tx, ts = partner(i)
        src, dst = ends(tx * 32 + ts)
        return pltpu.make_async_remote_copy(
            src_ref=src, dst_ref=dst, send_sem=ssem.at[i], recv_sem=rsem.at[i],
            device_id=(tx, ts), device_id_type=MESH)

    def start(i, c):
        copy(i).start()
        return c

    def wait(i, c):
        copy(i).wait()
        return c

    lax.fori_loop(1, NDEV, start, 0)
    own.wait()
    lax.fori_loop(1, NDEV, wait, 0)


ANY = pl.BlockSpec(memory_space=pl.ANY)
VM = pl.BlockSpec(memory_space=pltpu.VMEM)
SM = pl.BlockSpec(memory_space=pltpu.SMEM)
LIMIT = 56 * 2**20


def exchange(x, shape, to_owner, name):
    return pl.pallas_call(
        functools.partial(exchange_kernel, to_owner),
        out_shape=jax.ShapeDtypeStruct(shape, BF),
        in_specs=[ANY],
        out_specs=ANY,
        scratch_shapes=[pltpu.SemaphoreType.DMA((NDEV,)), pltpu.SemaphoreType.DMA((NDEV,)), pltpu.SemaphoreType.DMA],
        compiler_params=pltpu.CompilerParams(has_side_effects=True),
        name=name,
    )(x)


def per_device(fields, depart, blend, wave_owner, damping):
    me = my_index()
    count = NDEV
    low = lax.ppermute(fields[ROWS - HALO:], ("band", "set"), [(i, i + 1) for i in range(count - 1)])
    high = lax.ppermute(fields[:HALO], ("band", "set"), [(i + 1, i) for i in range(count - 1)])
    m1, m2 = wave_owner % 20, wave_owner // 20
    grp = jnp.where(m1 == 10, 0, jnp.minimum(m1, 20 - m1) % 20)
    nat = (grp * 128 + jnp.where(m1 >= 10, 64, 0) + m2).astype(jnp.int32)[:, None]
    owned = lax.dynamic_slice_in_dim(wave_owner, me * OWN, OWN, 0)
    wave_lane = jnp.pad(jnp.repeat(owned, 32), (0, COLS - 32 * OWN), constant_values=MM)[None, :]
    damp_lane = jnp.tile(damping, COLS // FL)[None, :]
    fwd_lat, bwd_lat = latitude_tables()
    sent = pl.pallas_call(
        grid_kernel,
        out_shape=jax.ShapeDtypeStruct((TQ, MM, 128), BF),
        in_specs=[ANY, ANY, ANY, SM, VM, VM, VM],
        out_specs=VM,
        scratch_shapes=[
            pltpu.VMEM((ROWS + 2 * HALO, NB, FL, BW), BF),
            pltpu.VMEM((20, FL, 256), F32),
            pltpu.VMEM((NG, ROWS * FL, 512), BF),
            pltpu.VMEM((ROWS, 2, FL, MM), BF),
            pltpu.VMEM((MM, MM), BF),
            pltpu.SemaphoreType.DMA((3 * NB,)),
        ],
        compiler_params=pltpu.CompilerParams(vmem_limit_bytes=LIMIT),
        name="grid_step",
    )(low, fields, high, depart.reshape(-1), blend, nat, jnp.asarray(forward_tables()))
    got = exchange(sent.reshape(TQ, MM // 2, 2, 128), (NDEV, TQ, 5, 2, 128), True, "to_owner")
    spectra, back = pl.pallas_call(
        lat_kernel,
        out_shape=(jax.ShapeDtypeStruct((OWN, FL, 2, MM), F32), jax.ShapeDtypeStruct((NDEV * 50, 128), BF)),
        in_specs=[VM] * 5,
        out_specs=(VM, VM),
        scratch_shapes=[
            pltpu.VMEM((NDEV * 50, 128), F32),
            pltpu.VMEM((2, NLAT // 2, COLS), BF),
            pltpu.VMEM((3 * MM, 128), F32),
            pltpu.VMEM((2, MM // 2, COLS), BF),
            pltpu.VMEM((NDEV * 50, 128), F32),
        ],
        compiler_params=pltpu.CompilerParams(vmem_limit_bytes=LIMIT),
        name="latitude_step",
    )(got.reshape(NDEV * 50, 128), jnp.asarray(fwd_lat), jnp.asarray(bwd_lat), damp_lane, wave_lane)
    zonal = exchange(back.reshape(NDEV, TQ, 5, 2, 128), (TQ, MM // 2, 2, 128), False, "to_cycles")
    updated = pl.pallas_call(
        wave_kernel,
        out_shape=jax.ShapeDtypeStruct((ROWS, FL, NLON), BF),
        in_specs=[VM] * 3,
        out_specs=VM,
        scratch_shapes=[
            pltpu.VMEM((ROWS * 32, MM), BF),
            pltpu.VMEM((MM, MM), BF),
            pltpu.VMEM((ROWS, 2, FL, MM), BF),
            pltpu.VMEM((NG, ROWS * FL, 512), F32),
        ],
        compiler_params=pltpu.CompilerParams(vmem_limit_bytes=LIMIT),
        name="wave_step",
    )(zonal.reshape(TQ, MM, 128), nat, jnp.asarray(inverse_tables()))
    return (updated, spectra)


def solution(mesh):
    in_specs = (
        P(("band", "set"), None, None),
        P(("band", "set"), None, None),
        P(("band", "set"), None, None, None),
        P(),
        P(),
    )
    out_specs = (P(("band", "set"), None, None), P(("band", "set"), None, None, None))
    return jax.shard_map(
        per_device, mesh=mesh, in_specs=in_specs, out_specs=out_specs, check_vma=False
    )
```

```python
import functools
import math

import jax
import jax.numpy as jnp
import ml_dtypes
import numpy as np
from jax import lax
from jax.experimental import pallas as pl
from jax.experimental.pallas import tpu as pltpu
from jax.sharding import PartitionSpec as P

NLAT = 2560
NLON = 5120
MM = 1280
LEV = 8
BW = 128
K = 4
HALO = 4
FL = 16
NB = 40
ROWS = 20
NDEV = 128
OWN = 10
TQ = 5
NG = 10
COLS = 384
MESH = pl.DeviceIdType.MESH
BF = jnp.bfloat16
F32 = jnp.float32


def group_waves(g):
    m2 = np.arange(64)
    if g == 0:
        return 20 * m2, 10 + 20 * m2
    return g + 20 * m2, 20 - g + 20 * m2


@functools.lru_cache(None)
def forward_tables():
    s = math.sqrt(2.0 / NLON)
    i = np.arange(256)
    out = np.zeros((NG, 512, 256))
    for g in range(NG):
        lo, hi = group_waves(g)
        for half, m in ((0, lo), (1, hi)):
            a = 2 * np.pi * ((i[:, None] * m[None, :]) % NLON) / NLON
            c, sn = s * np.cos(a), s * np.sin(a)
            re = slice(64 * half, 64 * half + 64)
            im = slice(128 + 64 * half, 192 + 64 * half)
            if g == 0:
                rows = slice(256 * half, 256 * half + 256)
                out[g, rows, re] = c
                out[g, rows, im] = -sn
            else:
                sign = 1.0 if half == 0 else -1.0
                out[g, :256, re] = c
                out[g, :256, im] = -sn
                out[g, 256:, re] = sign * sn
                out[g, 256:, im] = sign * c
    return out.astype(ml_dtypes.bfloat16)


@functools.lru_cache(None)
def inverse_tables():
    s = math.sqrt(2.0 / NLON)
    i = np.arange(256)
    out = np.zeros((NG, 256, 512))
    for g in range(NG):
        lo, hi = group_waves(g)
        for half, m in ((0, lo), (1, hi)):
            a = 2 * np.pi * ((m[:, None] * i[None, :]) % NLON) / NLON
            w = np.where(m == 0, 0.5, 1.0)[:, None] * s
            c, sn = w * np.cos(a), w * np.sin(a)
            re = slice(64 * half, 64 * half + 64)
            im = slice(128 + 64 * half, 192 + 64 * half)
            if g == 0:
                cols = slice(256 * half, 256 * half + 256)
                out[g, re, cols] = c
                out[g, im, cols] = -sn
            else:
                sign = 1.0 if half == 0 else -1.0
                out[g, re, :256] = c
                out[g, im, :256] = -sn
                out[g, re, 256:] = sign * sn
                out[g, im, 256:] = sign * c
    return out.astype(ml_dtypes.bfloat16)


@functools.lru_cache(None)
def latitude_tables():
    c, t, r, sl = np.meshgrid(np.arange(4), np.arange(TQ), np.arange(4), np.arange(16), indexing="ij")
    j = (20 * (4 * sl + c) + 4 * t + r).reshape(-1)
    n = np.arange(MM)
    g = np.where(n == 0, math.sqrt(1.0 / NLAT), math.sqrt(2.0 / NLAT))
    b = g[:, None] * np.cos(np.pi * ((n[:, None] * (2 * j[None, :] + 1)) % (4 * NLAT)) / (2 * NLAT))
    be, bo = b[0::2], b[1::2]
    fwd = np.stack([be, bo]).astype(ml_dtypes.bfloat16)
    bwd = np.stack([be.T, bo.T]).astype(ml_dtypes.bfloat16)
    return np.ascontiguousarray(fwd), np.ascontiguousarray(bwd)


C1, C2 = math.cos(2 * math.pi / 5), math.cos(4 * math.pi / 5)
S1, S2 = math.sin(2 * math.pi / 5), math.sin(4 * math.pi / 5)


def five_parts(x):
    e1, e2 = x[1] + x[4], x[2] + x[3]
    o1, o2 = x[1] - x[4], x[2] - x[3]
    total = x[0] + (e1 + e2)
    return total, x[0] + C1 * e1 + C2 * e2, x[0] + C2 * e1 + C1 * e2, S1 * o1 + S2 * o2, S2 * o1 - S1 * o2


def dft20(d):
    alpha, beta, gr, gi = [], [], [], []
    for q in range(5):
        v = [None] * 4
        for b in (q, q + 5, q + 10, q + 15):
            v[b % 4] = d[b]
        e, o = v[0] + v[2], v[1] + v[3]
        alpha.append(e + o)
        beta.append(e - o)
        gr.append(v[0] - v[2])
        gi.append(v[3] - v[1])
    out = [None] * 11
    s, e1, e2, o1, o2 = five_parts(alpha)
    out[0], out[4], out[8] = (s, None), (e1, -o1), (e2, -o2)
    s, e1, e2, o1, o2 = five_parts(beta)
    out[10], out[6], out[2] = (s, None), (e1, o1), (e2, o2)
    s, e1, e2, o1, o2 = five_parts(gr)
    t, f1, f2, p1, p2 = five_parts(gi)
    out[5] = (s, t)
    out[9] = (e1 + p1, f1 - o1)
    out[1] = (e1 - p1, f1 + o1)
    out[7] = (e2 + p2, o2 - f2)
    out[3] = (e2 - p2, -(f2 + o2))
    return out


def idft20(c):
    a, bb, dr, di = [], [], [], []

    def spread(x0, pr, mi):
        ev1 = x0 + C1 * pr[0] + C2 * pr[1]
        ev2 = x0 + C2 * pr[0] + C1 * pr[1]
        od1 = S1 * mi[0] + S2 * mi[1]
        od2 = S2 * mi[0] - S1 * mi[1]
        return [x0 + (pr[0] + pr[1]), ev1 + od1, ev2 + od2, ev2 - od2, ev1 - od1]

    a = spread(c[0][0], (c[4][0], c[8][0]), (-c[4][1], -c[8][1]))
    bb = spread(c[10][0], (c[6][0], c[2][0]), (c[6][1], c[2][1]))
    dr = spread(
        c[5][0],
        (c[1][0] + c[9][0], c[3][0] + c[7][0]),
        (c[1][1] - c[9][1], c[7][1] - c[3][1]),
    )
    di = spread(
        c[5][1],
        (c[1][1] + c[9][1], -(c[3][1] + c[7][1])),
        (c[9][0] - c[1][0], c[7][0] - c[3][0]),
    )
    plus = [a[q] + bb[q] for q in range(5)]
    minus = [a[q] - bb[q] for q in range(5)]
    out = []
    for b in range(20):
        q = b % 5
        base = plus[q] if b % 2 == 0 else minus[q]
        r = b % 4
        out.append(base + dr[q] if r == 0 else base - di[q] if r == 1 else base - dr[q] if r == 2 else base + di[q])
    return out


def my_index():
    return lax.axis_index("band") * 32 + lax.axis_index("set")


def local_row(me, p):
    return jnp.where(me < NDEV // 2, p, ROWS - 1 - p)


def place_of(d):
    far = d // (NDEV // 2)
    s = d + far * (NDEV - 1 - 2 * d)
    return far * 64 + (s % 4) * 16 + s // 4


def nat_columns(wave_ref, out_ref):
    w = wave_ref[...]
    m2 = w // 20
    m1 = w - 20 * m2
    grp = jnp.where(m1 > 10, 20 - m1, jnp.where(m1 == 10, 0, m1))
    nat = (grp * 128 + jnp.where(m1 >= 10, 64, 0) + m2).astype(F32)
    for i in range(MM // 128):
        out_ref[pl.ds(i * 128, 128), :] = jnp.transpose(
            jnp.broadcast_to(nat[:, i * 128:(i + 1) * 128], (128, 128)))


def one_hot(nat, first, count):
    lanes = first + lax.broadcasted_iota(jnp.int32, nat.shape, 1).astype(F32)
    return jnp.concatenate(
        [jnp.where(nat == lanes + 128.0 * j, 1.0, 0.0).astype(BF) for j in range(count // 128)], axis=1)


def device_of(index):
    return index // 32, index % 32


def grid_kernel(fields_ref, dep_ref, blend_hbm, tab_hbm, out_ref,
                mid, top, low, blend_v, tab_v, dep_f, g_buf, sem, big_sem, send_sem, recv_sem):
    me = my_index()
    right, left = (me + 1) % NDEV, (me + NDEV - 1) % NDEV
    barrier = pltpu.get_barrier_semaphore()
    for d in (left, right):
        pl.semaphore_signal(barrier, inc=1, device_id=device_of(d), device_id_type=MESH)
    parts = []
    for part, (first, count, ref, at) in enumerate(((0, 2 * HALO, top, HALO), (ROWS - 2 * HALO, 2 * HALO, low, 0), (0, ROWS, mid, 0))):
        parts.append([pltpu.make_async_copy(
            fields_ref.at[pl.ds(first, count), :, pl.ds(b * BW, BW)],
            ref.at[pl.ds(at, count), b], sem.at[part * NB + b]) for b in range(NB)])
    for c in parts[0] + parts[1]:
        c.start()
    load_blend = pltpu.make_async_copy(blend_hbm, blend_v, big_sem.at[0])
    load_blend.start()
    for c in parts[2]:
        c.start()
    load_tab = pltpu.make_async_copy(tab_hbm, tab_v, big_sem.at[1])
    load_tab.start()
    for c in parts[0] + parts[1]:
        c.wait()
    pl.semaphore_wait(barrier, 2)
    halos = []
    for i, (src, dst, d) in enumerate(((low.at[pl.ds(HALO, HALO)], top.at[pl.ds(0, HALO)], right),
                                       (top.at[pl.ds(HALO, HALO)], low.at[pl.ds(2 * HALO, HALO)], left))):
        halos.append(pltpu.make_async_remote_copy(
            src_ref=src, dst_ref=dst, send_sem=send_sem.at[i], recv_sem=recv_sem.at[i],
            device_id=device_of(d), device_id_type=MESH))
    for c in halos:
        c.start()
    load_blend.wait()
    for c in parts[2]:
        c.wait()

    def cycles(first, count, ref):
        blocks = ref.reshape(ref.shape[0] * NB, FL, BW)

        def cycle(r, carry):
            p = local_row(me, r)
            for b in range(NB):
                total = None
                for k in range(K):
                    at = dep_ref[(r * NB + b) * K + k]
                    term = blend_v[r, b, pl.ds(k, 1), :] * blocks[at].astype(F32)
                    total = term if total is None else total + term
                dep_f[b // 2, :, pl.ds((b % 2) * BW, BW)] = total
            rows = pl.ds(pl.multiple_of(p * FL, FL), FL)
            for half in range(2):
                lanes = pl.ds(half * 128, 128)
                g = dft20([dep_f[b, :, lanes] for b in range(20)])
                pairs = [(g[0][0], g[10][0])] + [g[i] for i in range(1, 10)]
                for i, (re, im) in enumerate(pairs):
                    g_buf[i, rows, pl.ds(half * 128, 128)] = re.astype(BF)
                    g_buf[i, rows, pl.ds(256 + half * 128, 128)] = im.astype(BF)
            return carry

        lax.fori_loop(first, first + count, cycle, 0)

    cycles(HALO, ROWS - 2 * HALO, mid)
    for c in halos:
        c.wait()
    cycles(0, HALO, top)
    cycles(ROWS - HALO, HALO, low)
    load_tab.wait()

    def group(g, carry):
        v = jnp.dot(g_buf[g], tab_v[g], preferred_element_type=F32).astype(BF)
        lanes = pl.ds(pl.multiple_of(g * 128, 128), 128)
        out_ref[:, 0, :, lanes] = v[:, :128].reshape(ROWS, FL, 128)
        out_ref[:, 1, :, lanes] = v[:, 128:].reshape(ROWS, FL, 128)
        return carry

    lax.fori_loop(0, NG, group, 0)


def block_swap(x):
    lane = lax.broadcasted_iota(jnp.int32, x[0].shape, 1)
    low64 = lane < 64
    low32 = (lane % 64) < 32
    z = [None] * 4
    for a in range(2):
        lo, hi = x[a], x[a + 2]
        z[a] = jnp.where(low64, lo, pltpu.roll(hi, 64, 1))
        z[a + 2] = jnp.where(low64, pltpu.roll(lo, 64, 1), hi)
    y = [None] * 4
    for a in (0, 2):
        lo, hi = z[a], z[a + 1]
        y[a] = jnp.where(low32, lo, pltpu.roll(hi, 32, 1))
        y[a + 1] = jnp.where(low32, pltpu.roll(lo, 96, 1), hi)
    return y


def partner(i):
    x = lax.axis_index("band")
    st = lax.axis_index("set")
    j = (i * 37) % NDEV
    tx = (x + j // 32) % 4
    ty = (st // 8 + (j // 8) % 4) % 4
    tz = ((st // 2) % 4 + (j // 2) % 4) % 4
    tc = (st % 2 + j % 2) % 2
    return tx, (ty * 4 + tz) * 2 + tc


def lat_kernel(f_ref, wave_v, wave_s, damp_s, fwd_hbm, bwd_hbm, out_ref, st_ref,
               natc, xs, rx, xf, uv, s16, zs, fwd_v, bwd_v, big_sem,
               send1, recv1, send2, recv2, own_sem):
    me = my_index()
    load_fwd = pltpu.make_async_copy(fwd_hbm, fwd_v, big_sem.at[0])
    load_bwd = pltpu.make_async_copy(bwd_hbm, bwd_v, big_sem.at[1])
    load_fwd.start()
    load_bwd.start()
    barrier = pltpu.get_barrier_semaphore()
    nat_columns(wave_v, natc)

    fourier = f_ref[...].reshape(ROWS * 32, MM)
    for i in range(MM // 256):
        for j in range(1 + 26 * i, min(27 + 26 * i, NDEV)):
            pl.semaphore_signal(barrier, inc=1, device_id=partner(j), device_id_type=MESH)
        v = lax.dot_general(one_hot(natc[pl.ds(i * 256, 256), :], 0.0, MM), fourier,
                            (((1,), (1,)), ((), ())), preferred_element_type=F32).astype(BF)
        for t in range(TQ):
            xs[t, pl.ds(i * 128, 128)] = v[:, t * 128:(t + 1) * 128].reshape(128, 2, 128)
    pl.semaphore_wait(barrier, NDEV - 1)

    def to_owner(i):
        tx, ts = partner(i)
        return pltpu.make_async_remote_copy(
            src_ref=xs.at[:, pl.ds((tx * 32 + ts) * 5, 5)], dst_ref=rx.at[place_of(me)],
            send_sem=send1.at[i], recv_sem=recv1.at[i], device_id=(tx, ts), device_id_type=MESH)

    def start(i, c):
        to_owner(i).start()
        return c

    def wait(i, c):
        to_owner(i).wait()
        return c

    lax.fori_loop(1, NDEV, start, 0)
    own = pltpu.make_async_copy(xs.at[:, pl.ds(me * 5, 5)], rx.at[place_of(me)], own_sem.at[0])
    own.start()
    own.wait()
    lax.fori_loop(1, NDEV, wait, 0)

    def widen(i, c):
        rows = pl.ds(pl.multiple_of(i * 400, 400), 400)
        xf[rows, :] = rx[pl.ds(i * 8, 8)].reshape(400, 128).astype(F32)
        return c

    lax.fori_loop(0, 16, widen, 0)

    def fold(i, carry):
        sc, t = i // TQ, i % TQ
        for g in range(3):
            us, vs = [], []
            for m in range(4 * g, 4 * g + 4):
                if m >= OWN:
                    us.append(jnp.zeros((16, 128), F32))
                    vs.append(jnp.zeros((16, 128), F32))
                    continue
                lo = xf[pl.ds(sc * 16 * 50 + t * OWN + m, 16, stride=50), :]
                hi = xf[pl.ds((64 + sc * 16) * 50 + t * OWN + m, 16, stride=50), :]
                us.append(lo + hi)
                vs.append(lo - hi)
            for par, vals in ((0, us), (1, vs)):
                y = block_swap(vals)
                for r in range(4):
                    rows = pl.ds(pl.multiple_of(i * 64 + r * 16, 16), 16)
                    uv[par, rows, pl.ds(g * 128, 128)] = y[r].astype(BF)
        return carry

    lax.fori_loop(0, 20, fold, 0)

    lane = lax.broadcasted_iota(jnp.int32, (1, COLS), 1)
    squared = (lane % FL) < LEV
    damp_row = jnp.zeros((1, COLS), F32)
    for f in range(FL):
        damp_row = jnp.where(lane % FL == f, damp_s[f], damp_row)
    wave_row = jnp.full((1, COLS), MM, jnp.int32)
    for m in range(OWN):
        wave_row = jnp.where(lane // 32 == m, wave_s[me * OWN + m], wave_row)
    load_fwd.wait()

    def analyse(i, carry):
        rows = pl.ds(pl.multiple_of(i * 128, 128), 128)
        for par in range(2):
            v = jnp.dot(fwd_v[par, rows, :], uv[par], preferred_element_type=F32)
            n = 2 * (i * 128 + lax.broadcasted_iota(jnp.int32, (128, COLS), 0)) + par
            nf = n.astype(F32)
            q = nf * (nf + 1.0) * (1.0 / (MM * (MM - 1.0)))
            qp = jnp.where(squared, q * q, q)
            v = v * (1.0 / (1.0 + damp_row * qp))
            v = jnp.where(n >= wave_row, v, 0.0)
            for g in range(3):
                st_ref[pl.ds(g * MM + i * 256 + par, 128, stride=2), :] = v[:, g * 128:(g + 1) * 128]
            s16[par, rows, :] = v.astype(BF)
        return carry

    lax.fori_loop(0, 5, analyse, 0)
    load_bwd.wait()
    turn = me % 4

    my_x, my_y, my_z = me // 32, (me // 8) % 4, (me // 4) % 2

    def to_cycles(place, d):
        return pltpu.make_async_remote_copy(
            src_ref=zs.at[place], dst_ref=out_ref.at[:, pl.ds(me * 5, 5)],
            send_sem=send2.at[place], recv_sem=recv2.at[me], device_id=device_of(d), device_id_type=MESH)

    keep = pltpu.make_async_copy(zs.at[place_of(me)], out_ref.at[:, pl.ds(me * 5, 5)], own_sem.at[1])

    def synth(i, carry):
        c = (i + turn) % 4
        rows = pl.ds(pl.multiple_of(c * 320, 320), 320)
        p = jnp.dot(bwd_v[0, rows, :], s16[0], preferred_element_type=F32)
        q = jnp.dot(bwd_v[1, rows, :], s16[1], preferred_element_type=F32)
        for half, z in ((0, p + q), (1, p - q)):
            first = (half * 64 + c * 16) * 50
            for t in range(TQ):
                for g in range(3):
                    y = block_swap([z[(t * 4 + r) * 16:(t * 4 + r + 1) * 16, g * 128:(g + 1) * 128] for r in range(4)])
                    for m in range(4 * g, min(4 * g + 4, OWN)):
                        xf[pl.ds(first + t * OWN + m, 16, stride=50), :] = y[m - 4 * g]
            zs[pl.ds(half * 64 + c * 16, 16)] = (
                xf[pl.ds(pl.multiple_of(first, 8), 800), :].astype(BF).reshape(16, TQ, 5, 2, 128))

        def send(j, carry):
            k = (j * 11) % 32
            tx, ty, tz = (my_x + k // 8) % 4, (my_y + (k // 2) % 4) % 4, (my_z + k % 2) % 2
            far = tx // 2
            d = tx * 32 + ty * 8 + tz * 4 + c + far * (3 - 2 * c)

            @pl.when(d != me)
            def _():
                to_cycles(place_of(d), d).start()

            @pl.when(d == me)
            def _():
                keep.start()

            return carry

        lax.fori_loop(0, 32, send, 0)
        return carry

    lax.fori_loop(0, 4, synth, 0)
    keep.wait()

    def finish(i, c):
        d = (me + i) % NDEV
        place = place_of(d)
        pltpu.make_async_remote_copy(
            src_ref=zs.at[place], dst_ref=out_ref.at[:, pl.ds(d * 5, 5)],
            send_sem=send2.at[place], recv_sem=recv2.at[d], device_id=device_of(d), device_id_type=MESH).wait()
        return c

    lax.fori_loop(1, NDEV, finish, 0)


def wave_kernel(x_ref, wave_v, st_ref, tab_hbm, out_hbm, spec_hbm,
                natc, hot, zt, zn, h_buf, tab_v, rows_v, spec_v, big_sem, row_sem):
    me = my_index()
    load_tab = pltpu.make_async_copy(tab_hbm, tab_v, big_sem.at[0])
    load_tab.start()
    nat_columns(wave_v, natc)

    def hots(i, c):
        rows = pl.ds(pl.multiple_of(i * 128, 128), 128)
        hot[rows, :] = one_hot(natc[rows, :], 0.0, MM)
        return c

    lax.fori_loop(0, MM // 128, hots, 0)

    def turn(t, carry):
        zt[pl.ds(pl.multiple_of(t * 128, 128), 128), :] = jnp.transpose(x_ref[t])
        return carry

    lax.fori_loop(0, TQ, turn, 0)

    def order(i, carry):
        lanes = pl.ds(pl.multiple_of(i * 256, 256), 256)
        v = jnp.dot(zt[...], hot[:, lanes], preferred_element_type=F32).astype(BF)
        zn[:, :, :, lanes] = v.reshape(ROWS, 2, FL, 256)
        return carry

    lax.fori_loop(0, MM // 256, order, 0)
    load_tab.wait()

    def group(g, carry):
        lanes = pl.ds(pl.multiple_of(g * 128, 128), 128)
        re = zn[:, 0, :, lanes].reshape(ROWS * FL, 128)
        im = zn[:, 1, :, lanes].reshape(ROWS * FL, 128)
        v = jnp.concatenate([re, im], axis=1)
        h_buf[g] = jnp.dot(v, tab_v[g], preferred_element_type=F32)
        return carry

    lax.fori_loop(0, NG, group, 0)

    def put(r):
        return pltpu.make_async_copy(rows_v.at[r], out_hbm.at[r], row_sem.at[r])

    def cycle(r, carry):
        rows = pl.ds(pl.multiple_of(local_row(me, r) * FL, FL), FL)
        for half in range(2):
            re = [h_buf[g, rows, pl.ds(half * 128, 128)] for g in range(NG)]
            im = [h_buf[g, rows, pl.ds(256 + half * 128, 128)] for g in range(NG)]
            c = [(re[0], None)] + [(re[g], im[g]) for g in range(1, NG)] + [(im[0], None)]
            y = idft20(c)
            for b in range(20):
                rows_v[r, :, pl.ds(b * 256 + half * 128, 128)] = y[b].astype(BF)
        put(r).start()
        return carry

    lax.fori_loop(0, ROWS, cycle, 0)

    for g in range(3):
        for nt in range(10):
            tr = jnp.transpose(st_ref[pl.ds(g * MM + nt * 128, 128), :])
            for m in range(4 * g, min(4 * g + 4, OWN)):
                for c in range(2):
                    first = (m - 4 * g) * 32 + c * 16
                    spec_v[m, :, c, pl.ds(nt * 128, 128)] = tr[first:first + 16]
    put_spec = pltpu.make_async_copy(spec_v, spec_hbm, big_sem.at[1])
    put_spec.start()

    def done(r, c):
        put(r).wait()
        return c

    lax.fori_loop(0, ROWS, done, 0)
    put_spec.wait()


ANY = pl.BlockSpec(memory_space=pl.ANY)
VM = pl.BlockSpec(memory_space=pltpu.VMEM)
SM = pl.BlockSpec(memory_space=pltpu.SMEM)
LIMIT = 56 * 2**20


def per_device(fields, depart, blend, wave_owner, damping):
    fwd_lat, bwd_lat = latitude_tables()
    dma = pltpu.SemaphoreType.DMA
    row = wave_owner.reshape(1, MM)
    r = jnp.arange(ROWS, dtype=jnp.int32)
    held = jnp.where(r < HALO, -HALO, jnp.where(r >= ROWS - HALO, ROWS - 2 * HALO, 0))
    places = (depart - ((my_index() * ROWS + held) * NB)[:, None, None]).reshape(-1)
    fourier = pl.pallas_call(
        grid_kernel,
        out_shape=jax.ShapeDtypeStruct((ROWS, 2, FL, MM), BF),
        in_specs=[ANY, SM, ANY, ANY],
        out_specs=VM,
        scratch_shapes=[
            pltpu.VMEM((ROWS, NB, FL, BW), BF),
            pltpu.VMEM((3 * HALO, NB, FL, BW), BF),
            pltpu.VMEM((3 * HALO, NB, FL, BW), BF),
            pltpu.VMEM((ROWS, NB, K, BW), F32),
            pltpu.VMEM((NG, 512, 256), BF),
            pltpu.VMEM((20, FL, 256), F32),
            pltpu.VMEM((NG, ROWS * FL, 512), BF),
            dma((3 * NB,)), dma((2,)), dma((2,)), dma((2,)),
        ],
        compiler_params=pltpu.CompilerParams(vmem_limit_bytes=LIMIT, collective_id=0, has_side_effects=True),
        name="grid_step",
    )(fields, places, blend, jnp.asarray(forward_tables()))
    zonal, st = pl.pallas_call(
        lat_kernel,
        out_shape=(jax.ShapeDtypeStruct((TQ, MM // 2, 2, 128), BF), jax.ShapeDtypeStruct((3 * MM, 128), F32)),
        in_specs=[VM, VM, SM, SM, ANY, ANY],
        out_specs=(ANY, VM),
        scratch_shapes=[
            pltpu.VMEM((MM, 128), F32),
            pltpu.VMEM((TQ, MM // 2, 2, 128), BF),
            pltpu.VMEM((NDEV, TQ, 5, 2, 128), BF),
            pltpu.VMEM((NDEV * 50, 128), F32),
            pltpu.VMEM((2, NLAT // 2, COLS), BF),
            pltpu.VMEM((2, MM // 2, COLS), BF),
            pltpu.VMEM((NDEV, TQ, 5, 2, 128), BF),
            pltpu.VMEM((2, MM // 2, NLAT // 2), BF),
            pltpu.VMEM((2, NLAT // 2, MM // 2), BF),
            dma((2,)), dma((NDEV,)), dma((NDEV,)), dma((NDEV,)), dma((NDEV,)), dma((2,)),
        ],
        compiler_params=pltpu.CompilerParams(vmem_limit_bytes=LIMIT, collective_id=1, has_side_effects=True),
        name="latitude_step",
    )(fourier, row, wave_owner, damping, jnp.asarray(fwd_lat), jnp.asarray(bwd_lat))
    updated, spectra = pl.pallas_call(
        wave_kernel,
        out_shape=(jax.ShapeDtypeStruct((ROWS, FL, NLON), BF), jax.ShapeDtypeStruct((OWN, FL, 2, MM), F32)),
        in_specs=[VM, VM, VM, ANY],
        out_specs=(ANY, ANY),
        scratch_shapes=[
            pltpu.VMEM((MM, 128), F32),
            pltpu.VMEM((MM, MM), BF),
            pltpu.VMEM((ROWS * 32, MM), BF),
            pltpu.VMEM((ROWS, 2, FL, MM), BF),
            pltpu.VMEM((NG, ROWS * FL, 512), F32),
            pltpu.VMEM((NG, 256, 512), BF),
            pltpu.VMEM((ROWS, FL, NLON), BF),
            pltpu.VMEM((OWN, FL, 2, MM), F32),
            dma((2,)), dma((ROWS,)),
        ],
        compiler_params=pltpu.CompilerParams(vmem_limit_bytes=LIMIT),
        name="wave_step",
    )(zonal.reshape(TQ, MM, 128), row, st, jnp.asarray(inverse_tables()))
    return (updated, spectra)


def solution(mesh):
    in_specs = (
        P(("band", "set"), None, None),
        P(("band", "set"), None, None),
        P(("band", "set"), None, None, None),
        P(),
        P(),
    )
    out_specs = (P(("band", "set"), None, None), P(("band", "set"), None, None, None))
    return jax.shard_map(
        per_device, mesh=mesh, in_specs=in_specs, out_specs=out_specs, check_vma=False
    )
```

```python
import functools
import math

import jax
import jax.numpy as jnp
import ml_dtypes
import numpy as np
from jax import lax
from jax.experimental import pallas as pl
from jax.experimental.pallas import tpu as pltpu
from jax.sharding import PartitionSpec as P

NLAT = 2560
NLON = 5120
MM = 1280
LEV = 8
BW = 128
K = 4
HALO = 4
FL = 16
NB = 40
ROWS = 20
NDEV = 128
OWN = 10
TQ = 5
NG = 10
COLS = 384
MESH = pl.DeviceIdType.MESH
BF = jnp.bfloat16
F32 = jnp.float32


def group_waves(g):
    m2 = np.arange(64)
    if g == 0:
        return 20 * m2, 10 + 20 * m2
    return g + 20 * m2, 20 - g + 20 * m2


@functools.lru_cache(None)
def forward_tables():
    s = math.sqrt(2.0 / NLON)
    i = np.arange(256)
    out = np.zeros((NG, 512, 256))
    for g in range(NG):
        lo, hi = group_waves(g)
        for half, m in ((0, lo), (1, hi)):
            a = 2 * np.pi * ((i[:, None] * m[None, :]) % NLON) / NLON
            c, sn = s * np.cos(a), s * np.sin(a)
            re = slice(64 * half, 64 * half + 64)
            im = slice(128 + 64 * half, 192 + 64 * half)
            if g == 0:
                rows = slice(256 * half, 256 * half + 256)
                out[g, rows, re] = c
                out[g, rows, im] = -sn
            else:
                sign = 1.0 if half == 0 else -1.0
                out[g, :256, re] = c
                out[g, :256, im] = -sn
                out[g, 256:, re] = sign * sn
                out[g, 256:, im] = sign * c
    return out.astype(ml_dtypes.bfloat16)


@functools.lru_cache(None)
def inverse_tables():
    s = math.sqrt(2.0 / NLON)
    i = np.arange(256)
    out = np.zeros((NG, 256, 512))
    for g in range(NG):
        lo, hi = group_waves(g)
        for half, m in ((0, lo), (1, hi)):
            a = 2 * np.pi * ((m[:, None] * i[None, :]) % NLON) / NLON
            w = np.where(m == 0, 0.5, 1.0)[:, None] * s
            c, sn = w * np.cos(a), w * np.sin(a)
            re = slice(64 * half, 64 * half + 64)
            im = slice(128 + 64 * half, 192 + 64 * half)
            if g == 0:
                cols = slice(256 * half, 256 * half + 256)
                out[g, re, cols] = c
                out[g, im, cols] = -sn
            else:
                sign = 1.0 if half == 0 else -1.0
                out[g, re, :256] = c
                out[g, im, :256] = -sn
                out[g, re, 256:] = sign * sn
                out[g, im, 256:] = sign * c
    return out.astype(ml_dtypes.bfloat16)


@functools.lru_cache(None)
def latitude_tables():
    c, t, r, sl = np.meshgrid(np.arange(4), np.arange(TQ), np.arange(4), np.arange(16), indexing="ij")
    j = (20 * (4 * sl + c) + 4 * t + r).reshape(-1)
    n = np.arange(MM)
    g = np.where(n == 0, math.sqrt(1.0 / NLAT), math.sqrt(2.0 / NLAT))
    b = g[:, None] * np.cos(np.pi * ((n[:, None] * (2 * j[None, :] + 1)) % (4 * NLAT)) / (2 * NLAT))
    be, bo = b[0::2], b[1::2]
    fwd = np.stack([be, bo]).astype(ml_dtypes.bfloat16)
    bwd = np.stack([be.T, bo.T]).astype(ml_dtypes.bfloat16)
    return np.ascontiguousarray(fwd), np.ascontiguousarray(bwd)


C1, C2 = math.cos(2 * math.pi / 5), math.cos(4 * math.pi / 5)
S1, S2 = math.sin(2 * math.pi / 5), math.sin(4 * math.pi / 5)


def five_parts(x):
    e1, e2 = x[1] + x[4], x[2] + x[3]
    o1, o2 = x[1] - x[4], x[2] - x[3]
    total = x[0] + (e1 + e2)
    return total, x[0] + C1 * e1 + C2 * e2, x[0] + C2 * e1 + C1 * e2, S1 * o1 + S2 * o2, S2 * o1 - S1 * o2


def dft20(d):
    alpha, beta, gr, gi = [], [], [], []
    for q in range(5):
        v = [None] * 4
        for b in (q, q + 5, q + 10, q + 15):
            v[b % 4] = d[b]
        e, o = v[0] + v[2], v[1] + v[3]
        alpha.append(e + o)
        beta.append(e - o)
        gr.append(v[0] - v[2])
        gi.append(v[3] - v[1])
    out = [None] * 11
    s, e1, e2, o1, o2 = five_parts(alpha)
    out[0], out[4], out[8] = (s, None), (e1, -o1), (e2, -o2)
    s, e1, e2, o1, o2 = five_parts(beta)
    out[10], out[6], out[2] = (s, None), (e1, o1), (e2, o2)
    s, e1, e2, o1, o2 = five_parts(gr)
    t, f1, f2, p1, p2 = five_parts(gi)
    out[5] = (s, t)
    out[9] = (e1 + p1, f1 - o1)
    out[1] = (e1 - p1, f1 + o1)
    out[7] = (e2 + p2, o2 - f2)
    out[3] = (e2 - p2, -(f2 + o2))
    return out


def idft20(c):
    a, bb, dr, di = [], [], [], []

    def spread(x0, pr, mi):
        ev1 = x0 + C1 * pr[0] + C2 * pr[1]
        ev2 = x0 + C2 * pr[0] + C1 * pr[1]
        od1 = S1 * mi[0] + S2 * mi[1]
        od2 = S2 * mi[0] - S1 * mi[1]
        return [x0 + (pr[0] + pr[1]), ev1 + od1, ev2 + od2, ev2 - od2, ev1 - od1]

    a = spread(c[0][0], (c[4][0], c[8][0]), (-c[4][1], -c[8][1]))
    bb = spread(c[10][0], (c[6][0], c[2][0]), (c[6][1], c[2][1]))
    dr = spread(
        c[5][0],
        (c[1][0] + c[9][0], c[3][0] + c[7][0]),
        (c[1][1] - c[9][1], c[7][1] - c[3][1]),
    )
    di = spread(
        c[5][1],
        (c[1][1] + c[9][1], -(c[3][1] + c[7][1])),
        (c[9][0] - c[1][0], c[7][0] - c[3][0]),
    )
    plus = [a[q] + bb[q] for q in range(5)]
    minus = [a[q] - bb[q] for q in range(5)]
    out = []
    for b in range(20):
        q = b % 5
        base = plus[q] if b % 2 == 0 else minus[q]
        r = b % 4
        out.append(base + dr[q] if r == 0 else base - di[q] if r == 1 else base - dr[q] if r == 2 else base + di[q])
    return out


def my_index():
    return lax.axis_index("band") * 32 + lax.axis_index("set")


def local_row(me, p):
    return jnp.where(me < NDEV // 2, p, ROWS - 1 - p)


def place_of(d):
    far = d // (NDEV // 2)
    s = d + far * (NDEV - 1 - 2 * d)
    return far * 64 + (s % 4) * 16 + s // 4


def nat_columns(wave_ref, out_ref):
    w = wave_ref[...]
    m2 = w // 20
    m1 = w - 20 * m2
    grp = jnp.where(m1 > 10, 20 - m1, jnp.where(m1 == 10, 0, m1))
    nat = (grp * 128 + jnp.where(m1 >= 10, 64, 0) + m2).astype(F32)
    for i in range(MM // 128):
        out_ref[pl.ds(i * 128, 128), :] = jnp.transpose(
            jnp.broadcast_to(nat[i:i + 1, :], (128, 128)))


def one_hot(nat, first, count):
    lanes = first + lax.broadcasted_iota(jnp.int32, nat.shape, 1).astype(F32)
    return jnp.concatenate(
        [jnp.where(nat == lanes + 128.0 * j, 1.0, 0.0).astype(BF) for j in range(count // 128)], axis=1)


def device_of(index):
    return index // 32, index % 32


def grid_kernel(fields_ref, dep_ref, blend_hbm, tab_hbm, out_ref,
                mid, top, low, blend_v, tab_v, dep_f, g_buf, sem, big_sem, send_sem, recv_sem):
    me = my_index()
    right, left = (me + 1) % NDEV, (me + NDEV - 1) % NDEV
    barrier = pltpu.get_barrier_semaphore()
    for d in (left, right):
        pl.semaphore_signal(barrier, inc=1, device_id=device_of(d), device_id_type=MESH)
    parts = []
    for part, (first, count, ref, at) in enumerate(((0, 2 * HALO, top, HALO), (ROWS - 2 * HALO, 2 * HALO, low, 0), (0, ROWS, mid, 0))):
        parts.append([pltpu.make_async_copy(
            fields_ref.at[pl.ds(first, count), :, pl.ds(b * BW, BW)],
            ref.at[pl.ds(at, count), b], sem.at[part * NB + b]) for b in range(NB)])
    for c in parts[0] + parts[1]:
        c.start()
    load_blend = pltpu.make_async_copy(blend_hbm, blend_v, big_sem.at[0])
    load_blend.start()
    for c in parts[2]:
        c.start()
    load_tab = pltpu.make_async_copy(tab_hbm, tab_v, big_sem.at[1])
    load_tab.start()
    for c in parts[0] + parts[1]:
        c.wait()
    pl.semaphore_wait(barrier, 2)
    halos = []
    for i, (src, dst, d) in enumerate(((low.at[pl.ds(HALO, HALO)], top.at[pl.ds(0, HALO)], right),
                                       (top.at[pl.ds(HALO, HALO)], low.at[pl.ds(2 * HALO, HALO)], left))):
        halos.append(pltpu.make_async_remote_copy(
            src_ref=src, dst_ref=dst, send_sem=send_sem.at[i], recv_sem=recv_sem.at[i],
            device_id=device_of(d), device_id_type=MESH))
    for c in halos:
        c.start()
    load_blend.wait()
    for c in parts[2]:
        c.wait()

    def cycles(first, count, ref):
        blocks = ref.reshape(ref.shape[0] * NB, FL, BW)

        def cycle(r, carry):
            p = local_row(me, r)
            for b in range(NB):
                total = None
                for k in range(K):
                    at = dep_ref[(r * NB + b) * K + k]
                    term = blend_v[r, b, pl.ds(k, 1), :] * blocks[at].astype(F32)
                    total = term if total is None else total + term
                dep_f[b // 2, :, pl.ds((b % 2) * BW, BW)] = total
            rows = pl.ds(pl.multiple_of(p * FL, FL), FL)
            for half in range(2):
                lanes = pl.ds(half * 128, 128)
                g = dft20([dep_f[b, :, lanes] for b in range(20)])
                pairs = [(g[0][0], g[10][0])] + [g[i] for i in range(1, 10)]
                for i, (re, im) in enumerate(pairs):
                    g_buf[i, rows, pl.ds(half * 128, 128)] = re.astype(BF)
                    g_buf[i, rows, pl.ds(256 + half * 128, 128)] = im.astype(BF)
            return carry

        lax.fori_loop(first, first + count, cycle, 0)

    def groups(spans):
        def group(g, carry):
            lanes = pl.ds(pl.multiple_of(g * 128, 128), 128)
            u = jnp.concatenate([g_buf[g, pl.ds(first * FL, count * FL), :] for first, count in spans], axis=0)
            v = jnp.dot(u, tab_v[g], preferred_element_type=F32).astype(BF)
            at = 0
            for first, count in spans:
                rows = v[at * FL:(at + count) * FL]
                out_ref[pl.ds(first, count), 0, :, lanes] = rows[:, :128].reshape(count, FL, 128)
                out_ref[pl.ds(first, count), 1, :, lanes] = rows[:, 128:].reshape(count, FL, 128)
                at += count
            return carry

        lax.fori_loop(0, NG, group, 0)

    cycles(HALO, ROWS - 2 * HALO, mid)
    load_tab.wait()
    groups(((HALO, ROWS - 2 * HALO),))
    for c in halos:
        c.wait()
    cycles(0, HALO, top)
    cycles(ROWS - HALO, HALO, low)
    groups(((0, HALO), (ROWS - HALO, HALO)))


def block_swap(x):
    lane = lax.broadcasted_iota(jnp.int32, x[0].shape, 1)
    low64 = lane < 64
    low32 = (lane % 64) < 32
    z = [None] * 4
    for a in range(2):
        lo, hi = x[a], x[a + 2]
        z[a] = jnp.where(low64, lo, pltpu.roll(hi, 64, 1))
        z[a + 2] = jnp.where(low64, pltpu.roll(lo, 64, 1), hi)
    y = [None] * 4
    for a in (0, 2):
        lo, hi = z[a], z[a + 1]
        y[a] = jnp.where(low32, lo, pltpu.roll(hi, 32, 1))
        y[a + 1] = jnp.where(low32, pltpu.roll(lo, 96, 1), hi)
    return y


def partner(i):
    x = lax.axis_index("band")
    st = lax.axis_index("set")
    j = (i * 37) % 64
    dz = j % 4
    tx = (x + j // 16) % 4
    ty = (st // 8 + (j // 4) % 4) % 4
    tz = ((st // 2) % 4 + dz) % 4
    tc = (st % 2 + dz + i // 64) % 2
    return tx, (ty * 4 + tz) * 2 + tc


def lat_kernel(f_ref, wave_v, wave_s, damp_s, fwd_hbm, bwd_hbm, out_ref, spec_hbm,
               st_ref, spec_v, natc, xs, rx, xf, uv, s16, zs, fwd_v, bwd_v, big_sem,
               send1, recv1, send2, recv2, own_sem):
    me = my_index()
    load_fwd = pltpu.make_async_copy(fwd_hbm, fwd_v, big_sem.at[0])
    load_bwd = pltpu.make_async_copy(bwd_hbm, bwd_v, big_sem.at[1])
    load_fwd.start()
    load_bwd.start()
    barrier = pltpu.get_barrier_semaphore()
    nat_columns(wave_v, natc)

    fourier = f_ref[...].reshape(ROWS * 32, MM)
    for i in range(MM // 256):
        for j in range(1 + 26 * i, min(27 + 26 * i, NDEV)):
            pl.semaphore_signal(barrier, inc=1, device_id=partner(j), device_id_type=MESH)
        v = lax.dot_general(one_hot(natc[pl.ds(i * 256, 256), :], 0.0, MM), fourier,
                            (((1,), (1,)), ((), ())), preferred_element_type=F32).astype(BF)
        for t in range(TQ):
            xs[t, pl.ds(i * 128, 128)] = v[:, t * 128:(t + 1) * 128].reshape(128, 2, 128)
    pl.semaphore_wait(barrier, NDEV - 1)

    def to_owner(i):
        tx, ts = partner(i)
        return pltpu.make_async_remote_copy(
            src_ref=xs.at[:, pl.ds((tx * 32 + ts) * 5, 5)], dst_ref=rx.at[place_of(me)],
            send_sem=send1.at[i], recv_sem=recv1.at[i], device_id=(tx, ts), device_id_type=MESH)

    def start(i, c):
        to_owner(i).start()
        return c

    def arrived(i, c):
        to_owner(i).wait_recv()
        return c

    def left(i, c):
        to_owner(i).wait_send()
        return c

    lax.fori_loop(1, NDEV, start, 0)
    own = pltpu.make_async_copy(xs.at[:, pl.ds(me * 5, 5)], rx.at[place_of(me)], own_sem.at[0])
    own.start()
    own.wait()
    def widen(sc):
        for half in range(2):
            first = half * 64 + sc * 16
            xf[pl.ds(pl.multiple_of(first * 50, 8), 800), :] = rx[pl.ds(first, 16)].reshape(800, 128).astype(F32)

    def fold(sc, t):
        for g in range(3):
            us, vs = [], []
            for m in range(4 * g, 4 * g + 4):
                if m >= OWN:
                    us.append(jnp.zeros((16, 128), F32))
                    vs.append(jnp.zeros((16, 128), F32))
                    continue
                lo = xf[pl.ds(sc * 16 * 50 + t * OWN + m, 16, stride=50), :]
                hi = xf[pl.ds((64 + sc * 16) * 50 + t * OWN + m, 16, stride=50), :]
                us.append(lo + hi)
                vs.append(lo - hi)
            for par, vals in ((0, us), (1, vs)):
                y = block_swap(vals)
                for r in range(4):
                    rows = pl.ds(pl.multiple_of((sc * TQ + t) * 64 + r * 16, 16), 16)
                    uv[par, rows, pl.ds(g * 128, 128)] = y[r].astype(BF)

    same = ((me // 2) + me) % 2
    for stage in range(2):
        lax.fori_loop(max(1, 64 * stage), 64 * stage + 64, arrived, 0)
        low = (same + stage) % 2

        def chunk(q, carry):
            sc = low + (q // TQ) * (3 - 2 * low)

            @pl.when(q % TQ == 0)
            def _():
                widen(sc)

            fold(sc, q % TQ)
            return carry

        lax.fori_loop(0, 2 * TQ, chunk, 0)

    lane = lax.broadcasted_iota(jnp.int32, (1, COLS), 1)
    squared = (lane % FL) < LEV
    damp_row = jnp.zeros((1, COLS), F32)
    for f in range(FL):
        damp_row = jnp.where(lane % FL == f, damp_s[f], damp_row)
    wave_row = jnp.full((1, COLS), MM, jnp.int32)
    for m in range(OWN):
        wave_row = jnp.where(lane // 32 == m, wave_s[me * OWN + m], wave_row)
    load_fwd.wait()

    def analyse(i, carry):
        rows = pl.ds(pl.multiple_of(i * 128, 128), 128)
        for par in range(2):
            v = jnp.dot(fwd_v[par, rows, :], uv[par], preferred_element_type=F32)
            n = 2 * (i * 128 + lax.broadcasted_iota(jnp.int32, (128, COLS), 0)) + par
            nf = n.astype(F32)
            q = nf * (nf + 1.0) * (1.0 / (MM * (MM - 1.0)))
            qp = jnp.where(squared, q * q, q)
            v = v * (1.0 / (1.0 + damp_row * qp))
            v = jnp.where(n >= wave_row, v, 0.0)
            for g in range(3):
                st_ref[pl.ds(g * MM + i * 256 + par, 128, stride=2), :] = v[:, g * 128:(g + 1) * 128]
            s16[par, rows, :] = v.astype(BF)
        return carry

    lax.fori_loop(0, 5, analyse, 0)
    load_bwd.wait()
    turn = me % 4

    my_x, my_y, my_z = me // 32, (me // 8) % 4, (me // 4) % 2

    def to_cycles(place, d):
        return pltpu.make_async_remote_copy(
            src_ref=zs.at[place], dst_ref=out_ref.at[:, pl.ds(me * 5, 5)],
            send_sem=send2.at[place], recv_sem=recv2.at[me], device_id=device_of(d), device_id_type=MESH)

    keep = pltpu.make_async_copy(zs.at[place_of(me)], out_ref.at[:, pl.ds(me * 5, 5)], own_sem.at[1])

    def synth(i, carry):
        c = (i + turn) % 4
        rows = pl.ds(pl.multiple_of(c * 320, 320), 320)
        p = jnp.dot(bwd_v[0, rows, :], s16[0], preferred_element_type=F32)
        q = jnp.dot(bwd_v[1, rows, :], s16[1], preferred_element_type=F32)
        for half, z in ((0, p + q), (1, p - q)):
            first = (half * 64 + c * 16) * 50
            for t in range(TQ):
                for g in range(3):
                    y = block_swap([z[(t * 4 + r) * 16:(t * 4 + r + 1) * 16, g * 128:(g + 1) * 128] for r in range(4)])
                    for m in range(4 * g, min(4 * g + 4, OWN)):
                        xf[pl.ds(first + t * OWN + m, 16, stride=50), :] = y[m - 4 * g]
            zs[pl.ds(half * 64 + c * 16, 16)] = (
                xf[pl.ds(pl.multiple_of(first, 8), 800), :].astype(BF).reshape(16, TQ, 5, 2, 128))

        def send(j, carry):
            k = (j * 11) % 32
            tx, ty, tz = (my_x + k // 8) % 4, (my_y + (k // 2) % 4) % 4, (my_z + k % 2) % 2
            far = tx // 2
            d = tx * 32 + ty * 8 + tz * 4 + c + far * (3 - 2 * c)

            @pl.when(d != me)
            def _():
                to_cycles(place_of(d), d).start()

            @pl.when(d == me)
            def _():
                keep.start()

            return carry

        lax.fori_loop(0, 32, send, 0)
        return carry

    lax.fori_loop(0, 4, synth, 0)
    for g in range(3):
        for nt in range(10):
            tr = jnp.transpose(st_ref[pl.ds(g * MM + nt * 128, 128), :])
            for m in range(4 * g, min(4 * g + 4, OWN)):
                for c in range(2):
                    first = (m - 4 * g) * 32 + c * 16
                    spec_v[m, :, c, pl.ds(nt * 128, 128)] = tr[first:first + 16]
    put_spec = pltpu.make_async_copy(spec_v, spec_hbm, big_sem.at[0])
    put_spec.start()
    keep.wait()
    lax.fori_loop(1, NDEV, left, 0)

    def finish(i, c):
        d = (me + i) % NDEV
        place = place_of(d)
        pltpu.make_async_remote_copy(
            src_ref=zs.at[place], dst_ref=out_ref.at[:, pl.ds(d * 5, 5)],
            send_sem=send2.at[place], recv_sem=recv2.at[d], device_id=device_of(d), device_id_type=MESH).wait()
        return c

    lax.fori_loop(1, NDEV, finish, 0)
    put_spec.wait()


def wave_kernel(x_ref, wave_v, tab_hbm, spec_in, out_hbm, spec_out,
                natc, hot, zt, zn, h_buf, tab_v, rows_v, spec_v, big_sem, row_sem):
    me = my_index()
    load_tab = pltpu.make_async_copy(tab_hbm, tab_v, big_sem.at[0])
    load_tab.start()
    take = pltpu.make_async_copy(spec_in, spec_v, big_sem.at[1])
    hand_on = pltpu.make_async_copy(spec_v, spec_out, big_sem.at[2])
    take.start()
    nat_columns(wave_v, natc)

    def hots(i, c):
        rows = pl.ds(pl.multiple_of(i * 128, 128), 128)
        hot[rows, :] = one_hot(natc[rows, :], 0.0, MM)
        return c

    lax.fori_loop(0, MM // 128, hots, 0)

    def turn(t, carry):
        zt[pl.ds(pl.multiple_of(t * 128, 128), 128), :] = jnp.transpose(x_ref[t])
        return carry

    lax.fori_loop(0, TQ, turn, 0)

    def order(i, carry):
        lanes = pl.ds(pl.multiple_of(i * 256, 256), 256)
        v = jnp.dot(zt[...], hot[:, lanes], preferred_element_type=F32).astype(BF)
        zn[:, :, :, lanes] = v.reshape(ROWS, 2, FL, 256)
        return carry

    lax.fori_loop(0, MM // 256, order, 0)
    load_tab.wait()
    take.wait()
    hand_on.start()

    def group(g, carry):
        lanes = pl.ds(pl.multiple_of(g * 128, 128), 128)
        re = zn[:, 0, :, lanes].reshape(ROWS * FL, 128)
        im = zn[:, 1, :, lanes].reshape(ROWS * FL, 128)
        v = jnp.concatenate([re, im], axis=1)
        h_buf[g] = jnp.dot(v, tab_v[g], preferred_element_type=F32)
        return carry

    lax.fori_loop(0, NG, group, 0)

    def put(r):
        return pltpu.make_async_copy(rows_v.at[r], out_hbm.at[r], row_sem.at[r])

    def cycle(r, carry):
        rows = pl.ds(pl.multiple_of(local_row(me, r) * FL, FL), FL)
        for half in range(2):
            re = [h_buf[g, rows, pl.ds(half * 128, 128)] for g in range(NG)]
            im = [h_buf[g, rows, pl.ds(256 + half * 128, 128)] for g in range(NG)]
            c = [(re[0], None)] + [(re[g], im[g]) for g in range(1, NG)] + [(im[0], None)]
            y = idft20(c)
            for b in range(20):
                rows_v[r, :, pl.ds(b * 256 + half * 128, 128)] = y[b].astype(BF)
        put(r).start()
        return carry

    lax.fori_loop(0, ROWS, cycle, 0)

    def done(r, c):
        put(r).wait()
        return c

    lax.fori_loop(0, ROWS, done, 0)
    hand_on.wait()

ANY = pl.BlockSpec(memory_space=pl.ANY)
VM = pl.BlockSpec(memory_space=pltpu.VMEM)
SM = pl.BlockSpec(memory_space=pltpu.SMEM)
LIMIT = 56 * 2**20


def per_device(fields, depart, blend, wave_owner, damping):
    fwd_lat, bwd_lat = latitude_tables()
    dma = pltpu.SemaphoreType.DMA
    row = wave_owner.reshape(MM // 128, 128)
    r = jnp.arange(ROWS, dtype=jnp.int32)
    held = jnp.where(r < HALO, -HALO, jnp.where(r >= ROWS - HALO, ROWS - 2 * HALO, 0))
    places = (depart - ((my_index() * ROWS + held) * NB)[:, None, None]).reshape(-1)
    fourier = pl.pallas_call(
        grid_kernel,
        out_shape=jax.ShapeDtypeStruct((ROWS, 2, FL, MM), BF),
        in_specs=[ANY, SM, ANY, ANY],
        out_specs=VM,
        scratch_shapes=[
            pltpu.VMEM((ROWS, NB, FL, BW), BF),
            pltpu.VMEM((3 * HALO, NB, FL, BW), BF),
            pltpu.VMEM((3 * HALO, NB, FL, BW), BF),
            pltpu.VMEM((ROWS, NB, K, BW), F32),
            pltpu.VMEM((NG, 512, 256), BF),
            pltpu.VMEM((20, FL, 256), F32),
            pltpu.VMEM((NG, ROWS * FL, 512), BF),
            dma((3 * NB,)), dma((2,)), dma((2,)), dma((2,)),
        ],
        compiler_params=pltpu.CompilerParams(vmem_limit_bytes=LIMIT, collective_id=0, has_side_effects=True),
        name="grid_step",
    )(fields, places, blend, jnp.asarray(forward_tables()))
    zonal, spectra = pl.pallas_call(
        lat_kernel,
        out_shape=(jax.ShapeDtypeStruct((TQ, MM // 2, 2, 128), BF), jax.ShapeDtypeStruct((OWN, FL, 2, MM), F32)),
        in_specs=[VM, VM, SM, SM, ANY, ANY],
        out_specs=(ANY, ANY),
        scratch_shapes=[
            pltpu.VMEM((3 * MM, 128), F32),
            pltpu.VMEM((OWN, FL, 2, MM), F32),
            pltpu.VMEM((MM, 128), F32),
            pltpu.VMEM((TQ, MM // 2, 2, 128), BF),
            pltpu.VMEM((NDEV, TQ, 5, 2, 128), BF),
            pltpu.VMEM((NDEV * 50, 128), F32),
            pltpu.VMEM((2, NLAT // 2, COLS), BF),
            pltpu.VMEM((2, MM // 2, COLS), BF),
            pltpu.VMEM((NDEV, TQ, 5, 2, 128), BF),
            pltpu.VMEM((2, MM // 2, NLAT // 2), BF),
            pltpu.VMEM((2, NLAT // 2, MM // 2), BF),
            dma((2,)), dma((NDEV,)), dma((NDEV,)), dma((NDEV,)), dma((NDEV,)), dma((2,)),
        ],
        compiler_params=pltpu.CompilerParams(vmem_limit_bytes=LIMIT, collective_id=1, has_side_effects=True),
        name="latitude_step",
    )(fourier, row, wave_owner, damping, jnp.asarray(fwd_lat), jnp.asarray(bwd_lat))
    updated, spectra = pl.pallas_call(
        wave_kernel,
        out_shape=(jax.ShapeDtypeStruct((ROWS, FL, NLON), BF), jax.ShapeDtypeStruct((OWN, FL, 2, MM), F32)),
        in_specs=[VM, VM, ANY, ANY],
        out_specs=(ANY, ANY),
        scratch_shapes=[
            pltpu.VMEM((MM, 128), F32),
            pltpu.VMEM((MM, MM), BF),
            pltpu.VMEM((ROWS * 32, MM), BF),
            pltpu.VMEM((ROWS, 2, FL, MM), BF),
            pltpu.VMEM((NG, ROWS * FL, 512), F32),
            pltpu.VMEM((NG, 256, 512), BF),
            pltpu.VMEM((ROWS, FL, NLON), BF),
            pltpu.VMEM((OWN, FL, 2, MM), F32),
            dma((3,)), dma((ROWS,)),
        ],
        compiler_params=pltpu.CompilerParams(vmem_limit_bytes=LIMIT),
        name="wave_step",
    )(zonal.reshape(TQ, MM, 128), row, jnp.asarray(inverse_tables()), spectra)
    return (updated, spectra)


def solution(mesh):
    in_specs = (
        P(("band", "set"), None, None),
        P(("band", "set"), None, None),
        P(("band", "set"), None, None, None),
        P(),
        P(),
    )
    out_specs = (P(("band", "set"), None, None), P(("band", "set"), None, None, None))
    return jax.shard_map(
        per_device, mesh=mesh, in_specs=in_specs, out_specs=out_specs, check_vma=False
    )
```

```python
import functools
import math

import jax
import jax.numpy as jnp
import ml_dtypes
import numpy as np
from jax import lax
from jax.experimental import pallas as pl
from jax.experimental.pallas import tpu as pltpu
from jax.sharding import PartitionSpec as P

NLAT = 2560
NLON = 5120
MM = 1280
LEV = 8
BW = 128
K = 4
HALO = 4
FL = 16
NB = 40
ROWS = 20
NDEV = 128
OWN = 10
TQ = 5
NG = 10
COLS = 384
MESH = pl.DeviceIdType.MESH
BF = jnp.bfloat16
F32 = jnp.float32


def group_waves(g):
    m2 = np.arange(64)
    if g == 0:
        return 20 * m2, 10 + 20 * m2
    return g + 20 * m2, 20 - g + 20 * m2


@functools.lru_cache(None)
def forward_tables():
    s = math.sqrt(2.0 / NLON)
    i = np.arange(256)
    out = np.zeros((NG, 512, 256))
    for g in range(NG):
        lo, hi = group_waves(g)
        for half, m in ((0, lo), (1, hi)):
            a = 2 * np.pi * ((i[:, None] * m[None, :]) % NLON) / NLON
            c, sn = s * np.cos(a), s * np.sin(a)
            re = slice(64 * half, 64 * half + 64)
            im = slice(128 + 64 * half, 192 + 64 * half)
            if g == 0:
                rows = slice(256 * half, 256 * half + 256)
                out[g, rows, re] = c
                out[g, rows, im] = -sn
            else:
                sign = 1.0 if half == 0 else -1.0
                out[g, :256, re] = c
                out[g, :256, im] = -sn
                out[g, 256:, re] = sign * sn
                out[g, 256:, im] = sign * c
    return out.astype(ml_dtypes.bfloat16)


@functools.lru_cache(None)
def inverse_tables():
    s = math.sqrt(2.0 / NLON)
    i = np.arange(256)
    out = np.zeros((NG, 256, 512))
    for g in range(NG):
        lo, hi = group_waves(g)
        for half, m in ((0, lo), (1, hi)):
            a = 2 * np.pi * ((m[:, None] * i[None, :]) % NLON) / NLON
            w = np.where(m == 0, 0.5, 1.0)[:, None] * s
            c, sn = w * np.cos(a), w * np.sin(a)
            re = slice(64 * half, 64 * half + 64)
            im = slice(128 + 64 * half, 192 + 64 * half)
            if g == 0:
                cols = slice(256 * half, 256 * half + 256)
                out[g, re, cols] = c
                out[g, im, cols] = -sn
            else:
                sign = 1.0 if half == 0 else -1.0
                out[g, re, :256] = c
                out[g, im, :256] = -sn
                out[g, re, 256:] = sign * sn
                out[g, im, 256:] = sign * c
    return out.astype(ml_dtypes.bfloat16)


@functools.lru_cache(None)
def latitude_tables():
    c, t, r, sl = np.meshgrid(np.arange(4), np.arange(TQ), np.arange(4), np.arange(16), indexing="ij")
    j = (20 * (4 * sl + c) + 4 * t + r).reshape(-1)
    n = np.arange(MM)
    g = np.where(n == 0, math.sqrt(1.0 / NLAT), math.sqrt(2.0 / NLAT))
    b = g[:, None] * np.cos(np.pi * ((n[:, None] * (2 * j[None, :] + 1)) % (4 * NLAT)) / (2 * NLAT))
    be, bo = b[0::2], b[1::2]
    fwd = np.stack([be, bo]).astype(ml_dtypes.bfloat16)
    bwd = np.stack([be.T, bo.T]).astype(ml_dtypes.bfloat16)
    return np.ascontiguousarray(fwd), np.ascontiguousarray(bwd)


C1, C2 = math.cos(2 * math.pi / 5), math.cos(4 * math.pi / 5)
S1, S2 = math.sin(2 * math.pi / 5), math.sin(4 * math.pi / 5)


def five_parts(x):
    e1, e2 = x[1] + x[4], x[2] + x[3]
    o1, o2 = x[1] - x[4], x[2] - x[3]
    total = x[0] + (e1 + e2)
    return total, x[0] + C1 * e1 + C2 * e2, x[0] + C2 * e1 + C1 * e2, S1 * o1 + S2 * o2, S2 * o1 - S1 * o2


def dft20(d):
    alpha, beta, gr, gi = [], [], [], []
    for q in range(5):
        v = [None] * 4
        for b in (q, q + 5, q + 10, q + 15):
            v[b % 4] = d[b]
        e, o = v[0] + v[2], v[1] + v[3]
        alpha.append(e + o)
        beta.append(e - o)
        gr.append(v[0] - v[2])
        gi.append(v[3] - v[1])
    out = [None] * 11
    s, e1, e2, o1, o2 = five_parts(alpha)
    out[0], out[4], out[8] = (s, None), (e1, -o1), (e2, -o2)
    s, e1, e2, o1, o2 = five_parts(beta)
    out[10], out[6], out[2] = (s, None), (e1, o1), (e2, o2)
    s, e1, e2, o1, o2 = five_parts(gr)
    t, f1, f2, p1, p2 = five_parts(gi)
    out[5] = (s, t)
    out[9] = (e1 + p1, f1 - o1)
    out[1] = (e1 - p1, f1 + o1)
    out[7] = (e2 + p2, o2 - f2)
    out[3] = (e2 - p2, -(f2 + o2))
    return out


def idft20(c):
    a, bb, dr, di = [], [], [], []

    def spread(x0, pr, mi):
        ev1 = x0 + C1 * pr[0] + C2 * pr[1]
        ev2 = x0 + C2 * pr[0] + C1 * pr[1]
        od1 = S1 * mi[0] + S2 * mi[1]
        od2 = S2 * mi[0] - S1 * mi[1]
        return [x0 + (pr[0] + pr[1]), ev1 + od1, ev2 + od2, ev2 - od2, ev1 - od1]

    a = spread(c[0][0], (c[4][0], c[8][0]), (-c[4][1], -c[8][1]))
    bb = spread(c[10][0], (c[6][0], c[2][0]), (c[6][1], c[2][1]))
    dr = spread(
        c[5][0],
        (c[1][0] + c[9][0], c[3][0] + c[7][0]),
        (c[1][1] - c[9][1], c[7][1] - c[3][1]),
    )
    di = spread(
        c[5][1],
        (c[1][1] + c[9][1], -(c[3][1] + c[7][1])),
        (c[9][0] - c[1][0], c[7][0] - c[3][0]),
    )
    plus = [a[q] + bb[q] for q in range(5)]
    minus = [a[q] - bb[q] for q in range(5)]
    out = []
    for b in range(20):
        q = b % 5
        base = plus[q] if b % 2 == 0 else minus[q]
        r = b % 4
        out.append(base + dr[q] if r == 0 else base - di[q] if r == 1 else base - dr[q] if r == 2 else base + di[q])
    return out


def my_index():
    return lax.axis_index("band") * 32 + lax.axis_index("set")


def local_row(me, p):
    return jnp.where(me < NDEV // 2, p, ROWS - 1 - p)


def place_of(d):
    far = d // (NDEV // 2)
    s = d + far * (NDEV - 1 - 2 * d)
    return far * 64 + (s % 4) * 16 + s // 4


def nat_columns(wave_ref, out_ref):
    w = wave_ref[...]
    m2 = w // 20
    m1 = w - 20 * m2
    grp = jnp.where(m1 > 10, 20 - m1, jnp.where(m1 == 10, 0, m1))
    nat = (grp * 128 + jnp.where(m1 >= 10, 64, 0) + m2).astype(F32)
    for i in range(MM // 128):
        out_ref[pl.ds(i * 128, 128), :] = jnp.transpose(
            jnp.broadcast_to(nat[i:i + 1, :], (128, 128)))


def one_hot(nat, first, count):
    lanes = first + lax.broadcasted_iota(jnp.int32, nat.shape, 1).astype(F32)
    return jnp.concatenate(
        [jnp.where(nat == lanes + 128.0 * j, 1.0, 0.0).astype(BF) for j in range(count // 128)], axis=1)


def device_of(index):
    return index // 32, index % 32


def grid_kernel(fields_ref, dep_ref, blend_hbm, tab_hbm, out_ref,
                mid, top, low, blend_v, tab_v, dep_f, g_buf, sem, big_sem, send_sem, recv_sem):
    me = my_index()
    right, left = (me + 1) % NDEV, (me + NDEV - 1) % NDEV
    barrier = pltpu.get_barrier_semaphore()
    for d in (left, right):
        pl.semaphore_signal(barrier, inc=1, device_id=device_of(d), device_id_type=MESH)
    parts = []
    for part, (first, count, ref, at) in enumerate(((0, 2 * HALO, top, HALO), (ROWS - 2 * HALO, 2 * HALO, low, 0), (0, ROWS, mid, 0))):
        parts.append([pltpu.make_async_copy(
            fields_ref.at[pl.ds(first, count), :, pl.ds(b * BW, BW)],
            ref.at[pl.ds(at, count), b], sem.at[part * NB + b]) for b in range(NB)])
    for c in parts[0] + parts[1]:
        c.start()
    load_blend = pltpu.make_async_copy(blend_hbm, blend_v, big_sem.at[0])
    load_blend.start()
    for c in parts[2]:
        c.start()
    load_tab = pltpu.make_async_copy(tab_hbm, tab_v, big_sem.at[1])
    load_tab.start()
    for c in parts[0] + parts[1]:
        c.wait()
    pl.semaphore_wait(barrier, 2)
    halos = []
    for i, (src, dst, d) in enumerate(((low.at[pl.ds(HALO, HALO)], top.at[pl.ds(0, HALO)], right),
                                       (top.at[pl.ds(HALO, HALO)], low.at[pl.ds(2 * HALO, HALO)], left))):
        halos.append(pltpu.make_async_remote_copy(
            src_ref=src, dst_ref=dst, send_sem=send_sem.at[i], recv_sem=recv_sem.at[i],
            device_id=device_of(d), device_id_type=MESH))
    for c in halos:
        c.start()
    load_blend.wait()
    for c in parts[2]:
        c.wait()

    def cycles(first, count, ref):
        blocks = ref.reshape(ref.shape[0] * NB, FL, BW)

        def cycle(r, carry):
            p = local_row(me, r)
            for b in range(NB):
                total = None
                for k in range(K):
                    at = dep_ref[(r * NB + b) * K + k]
                    term = blend_v[r, b, pl.ds(k, 1), :] * blocks[at].astype(F32)
                    total = term if total is None else total + term
                dep_f[b // 2, :, pl.ds((b % 2) * BW, BW)] = total
            rows = pl.ds(pl.multiple_of(p * FL, FL), FL)
            for half in range(2):
                lanes = pl.ds(half * 128, 128)
                g = dft20([dep_f[b, :, lanes] for b in range(20)])
                pairs = [(g[0][0], g[10][0])] + [g[i] for i in range(1, 10)]
                for i, (re, im) in enumerate(pairs):
                    g_buf[i, rows, pl.ds(half * 128, 128)] = re.astype(BF)
                    g_buf[i, rows, pl.ds(256 + half * 128, 128)] = im.astype(BF)
            return carry

        lax.fori_loop(first, first + count, cycle, 0)

    def groups(spans):
        def group(g, carry):
            lanes = pl.ds(pl.multiple_of(g * 128, 128), 128)
            u = jnp.concatenate([g_buf[g, pl.ds(first * FL, count * FL), :] for first, count in spans], axis=0)
            v = jnp.dot(u, tab_v[g], preferred_element_type=F32).astype(BF)
            at = 0
            for first, count in spans:
                rows = v[at * FL:(at + count) * FL]
                out_ref[pl.ds(first, count), 0, :, lanes] = rows[:, :128].reshape(count, FL, 128)
                out_ref[pl.ds(first, count), 1, :, lanes] = rows[:, 128:].reshape(count, FL, 128)
                at += count
            return carry

        lax.fori_loop(0, NG, group, 0)

    cycles(HALO, ROWS - 2 * HALO, mid)
    load_tab.wait()
    groups(((HALO, ROWS - 2 * HALO),))
    for c in halos:
        c.wait()
    cycles(0, HALO, top)
    cycles(ROWS - HALO, HALO, low)
    groups(((0, HALO), (ROWS - HALO, HALO)))


def block_swap(x):
    lane = lax.broadcasted_iota(jnp.int32, x[0].shape, 1)
    low64 = lane < 64
    low32 = (lane % 64) < 32
    z = [None] * 4
    for a in range(2):
        lo, hi = x[a], x[a + 2]
        z[a] = jnp.where(low64, lo, pltpu.roll(hi, 64, 1))
        z[a + 2] = jnp.where(low64, pltpu.roll(lo, 64, 1), hi)
    y = [None] * 4
    for a in (0, 2):
        lo, hi = z[a], z[a + 1]
        y[a] = jnp.where(low32, lo, pltpu.roll(hi, 32, 1))
        y[a + 1] = jnp.where(low32, pltpu.roll(lo, 96, 1), hi)
    return y


def partner(i):
    x = lax.axis_index("band")
    st = lax.axis_index("set")
    q, u = i // 32, (i * 11) % 32
    tx = (x + u // 8) % 4
    ty = (st // 8 + (u // 2) % 4) % 4
    tz = ((st // 2) % 4 + 2 * (u % 2) + q % 2) % 4
    tc = (st % 2 + (q + 1) // 2) % 2
    return tx, (ty * 4 + tz) * 2 + tc


def lat_kernel(f_ref, wave_v, wave_s, damp_s, fwd_hbm, bwd_hbm, out_ref, spec_hbm,
               st_ref, spec_v, natc, natq, xs, rx, xf, uv, s16, zs, fwd_v, bwd_v, big_sem,
               send1, recv1, send2, recv2, own_sem):
    me = my_index()
    load_fwd = pltpu.make_async_copy(fwd_hbm, fwd_v, big_sem.at[0])
    load_bwd = pltpu.make_async_copy(bwd_hbm, bwd_v, big_sem.at[1])
    load_fwd.start()
    load_bwd.start()
    barrier = pltpu.get_barrier_semaphore()
    nat_columns(wave_v, natc)

    for j in range(1, NDEV):
        pl.semaphore_signal(barrier, inc=1, device_id=partner(j), device_id_type=MESH)
    for q in range(4):
        for m in range(OWN):
            natq[pl.ds(q * 320 + m, 32, stride=OWN), :] = natc[pl.ds(q * OWN + m, 32, stride=4 * OWN), :]
    fourier = f_ref[...].reshape(ROWS * 32, MM)

    def place_sent(d):
        return pl.ds(((d % 4) * 32 + d // 4) * 5, 5)

    def to_owner(i):
        tx, ts = partner(i)
        return pltpu.make_async_remote_copy(
            src_ref=xs.at[:, place_sent(tx * 32 + ts)], dst_ref=rx.at[place_of(me)],
            send_sem=send1.at[i], recv_sem=recv1.at[i], device_id=(tx, ts), device_id_type=MESH)

    def arrived(i, c):
        to_owner(i).wait_recv()
        return c

    def left(i, c):
        to_owner(i).wait_send()
        return c

    own = pltpu.make_async_copy(xs.at[:, place_sent(me)], rx.at[place_of(me)], own_sem.at[0])
    low2 = me % 4
    flip = low2 + 1 - 2 * (low2 % 2)
    for q, bits in enumerate((low2, 3 - low2, flip, 3 - flip)):
        v = lax.dot_general(one_hot(natq[pl.ds(pl.multiple_of(bits * 320, 64), 320), :], 0.0, MM), fourier,
                            (((1,), (1,)), ((), ())), preferred_element_type=F32).astype(BF)
        for t in range(TQ):
            xs[t, pl.ds(bits * 160, 160)] = v[:, t * 128:(t + 1) * 128].reshape(160, 2, 128)
        if q == 0:
            pl.semaphore_wait(barrier, NDEV - 1)
            own.start()
        for i in range(max(1, 32 * q), 32 * q + 32):
            to_owner(i).start()
    own.wait()

    def widen(sc):
        for half in range(2):
            first = half * 64 + sc * 16
            xf[pl.ds(pl.multiple_of(first * 50, 8), 800), :] = rx[pl.ds(first, 16)].reshape(800, 128).astype(F32)

    def fold(sc, t):
        for g in range(3):
            us, vs = [], []
            for m in range(4 * g, 4 * g + 4):
                if m >= OWN:
                    us.append(jnp.zeros((16, 128), F32))
                    vs.append(jnp.zeros((16, 128), F32))
                    continue
                lo = xf[pl.ds(sc * 16 * 50 + t * OWN + m, 16, stride=50), :]
                hi = xf[pl.ds((64 + sc * 16) * 50 + t * OWN + m, 16, stride=50), :]
                us.append(lo + hi)
                vs.append(lo - hi)
            for par, vals in ((0, us), (1, vs)):
                y = block_swap(vals)
                for r in range(4):
                    rows = pl.ds(pl.multiple_of((sc * TQ + t) * 64 + r * 16, 16), 16)
                    uv[par, rows, pl.ds(g * 128, 128)] = y[r].astype(BF)

    same = ((me // 2) + me) % 2
    for stage in range(2):
        lax.fori_loop(max(1, 64 * stage), 64 * stage + 64, arrived, 0)
        low = (same + stage) % 2

        def chunk(q, carry):
            sc = low + (q // TQ) * (3 - 2 * low)

            @pl.when(q % TQ == 0)
            def _():
                widen(sc)

            fold(sc, q % TQ)
            return carry

        lax.fori_loop(0, 2 * TQ, chunk, 0)

    lane = lax.broadcasted_iota(jnp.int32, (1, COLS), 1)
    squared = (lane % FL) < LEV
    damp_row = jnp.zeros((1, COLS), F32)
    for f in range(FL):
        damp_row = jnp.where(lane % FL == f, damp_s[f], damp_row)
    wave_row = jnp.full((1, COLS), MM, jnp.int32)
    for m in range(OWN):
        wave_row = jnp.where(lane // 32 == m, wave_s[me * OWN + m], wave_row)
    load_fwd.wait()

    def analyse(i, carry):
        rows = pl.ds(pl.multiple_of(i * 128, 128), 128)
        for par in range(2):
            v = jnp.dot(fwd_v[par, rows, :], uv[par], preferred_element_type=F32)
            n = 2 * (i * 128 + lax.broadcasted_iota(jnp.int32, (128, COLS), 0)) + par
            nf = n.astype(F32)
            q = nf * (nf + 1.0) * (1.0 / (MM * (MM - 1.0)))
            qp = jnp.where(squared, q * q, q)
            v = v * (1.0 / (1.0 + damp_row * qp))
            v = jnp.where(n >= wave_row, v, 0.0)
            for g in range(3):
                st_ref[pl.ds(g * MM + i * 256 + par, 128, stride=2), :] = v[:, g * 128:(g + 1) * 128]
            s16[par, rows, :] = v.astype(BF)
        return carry

    lax.fori_loop(0, 5, analyse, 0)
    load_bwd.wait()
    turn = me % 4

    my_x, my_y, my_z = me // 32, (me // 8) % 4, (me // 4) % 2

    def to_cycles(place, d):
        return pltpu.make_async_remote_copy(
            src_ref=zs.at[place], dst_ref=out_ref.at[:, pl.ds(me * 5, 5)],
            send_sem=send2.at[place], recv_sem=recv2.at[me], device_id=device_of(d), device_id_type=MESH)

    keep = pltpu.make_async_copy(zs.at[place_of(me)], out_ref.at[:, pl.ds(me * 5, 5)], own_sem.at[1])

    def synth(i, carry):
        c = (i + turn) % 4
        rows = pl.ds(pl.multiple_of(c * 320, 320), 320)
        p = jnp.dot(bwd_v[0, rows, :], s16[0], preferred_element_type=F32)
        q = jnp.dot(bwd_v[1, rows, :], s16[1], preferred_element_type=F32)
        for half, z in ((0, p + q), (1, p - q)):
            first = (half * 64 + c * 16) * 50
            for t in range(TQ):
                for g in range(3):
                    y = block_swap([z[(t * 4 + r) * 16:(t * 4 + r + 1) * 16, g * 128:(g + 1) * 128] for r in range(4)])
                    for m in range(4 * g, min(4 * g + 4, OWN)):
                        xf[pl.ds(first + t * OWN + m, 16, stride=50), :] = y[m - 4 * g]
            zs[pl.ds(half * 64 + c * 16, 16)] = (
                xf[pl.ds(pl.multiple_of(first, 8), 800), :].astype(BF).reshape(16, TQ, 5, 2, 128))

        for j in range(32):
            k = (j * 11) % 32
            tx, ty, tz = (my_x + k // 8) % 4, (my_y + (k // 2) % 4) % 4, (my_z + k % 2) % 2
            far = tx // 2
            low_bits = c + far * (3 - 2 * c)
            d = tx * 32 + ty * 8 + tz * 4 + low_bits
            place = far * 64 + c * 16 + (d // 4 + far * (31 - 2 * (d // 4)))
            if k > 0:
                to_cycles(place, d).start()
                continue

            @pl.when(d != me)
            def _():
                to_cycles(place, d).start()

            @pl.when(d == me)
            def _():
                keep.start()

        return carry

    lax.fori_loop(0, 4, synth, 0)
    for g in range(3):
        for nt in range(10):
            tr = jnp.transpose(st_ref[pl.ds(g * MM + nt * 128, 128), :])
            for m in range(4 * g, min(4 * g + 4, OWN)):
                for c in range(2):
                    first = (m - 4 * g) * 32 + c * 16
                    spec_v[m, :, c, pl.ds(nt * 128, 128)] = tr[first:first + 16]
    put_spec = pltpu.make_async_copy(spec_v, spec_hbm, big_sem.at[0])
    put_spec.start()
    keep.wait()
    lax.fori_loop(1, NDEV, left, 0)

    def finish(i, c):
        d = (me + i) % NDEV
        place = place_of(d)
        pltpu.make_async_remote_copy(
            src_ref=zs.at[place], dst_ref=out_ref.at[:, pl.ds(d * 5, 5)],
            send_sem=send2.at[place], recv_sem=recv2.at[d], device_id=device_of(d), device_id_type=MESH).wait()
        return c

    lax.fori_loop(1, NDEV, finish, 0)
    put_spec.wait()


def wave_kernel(x_ref, wave_v, tab_hbm, spec_in, out_hbm, spec_out,
                natc, hot, zt, zn, h_buf, tab_v, rows_v, spec_v, big_sem, row_sem):
    me = my_index()
    load_tab = pltpu.make_async_copy(tab_hbm, tab_v, big_sem.at[0])
    load_tab.start()
    take = pltpu.make_async_copy(spec_in, spec_v, big_sem.at[1])
    hand_on = pltpu.make_async_copy(spec_v, spec_out, big_sem.at[2])
    take.start()
    nat_columns(wave_v, natc)

    def hots(i, c):
        rows = pl.ds(pl.multiple_of(i * 128, 128), 128)
        hot[rows, :] = one_hot(natc[rows, :], 0.0, MM)
        return c

    lax.fori_loop(0, MM // 128, hots, 0)

    def turn(t, carry):
        zt[pl.ds(pl.multiple_of(t * 128, 128), 128), :] = jnp.transpose(x_ref[t])
        return carry

    lax.fori_loop(0, TQ, turn, 0)

    def order(i, carry):
        lanes = pl.ds(pl.multiple_of(i * 256, 256), 256)
        v = jnp.dot(zt[...], hot[:, lanes], preferred_element_type=F32).astype(BF)
        zn[:, :, :, lanes] = v.reshape(ROWS, 2, FL, 256)
        return carry

    lax.fori_loop(0, MM // 256, order, 0)
    load_tab.wait()
    take.wait()
    hand_on.start()

    def group(g, carry):
        lanes = pl.ds(pl.multiple_of(g * 128, 128), 128)
        re = zn[:, 0, :, lanes].reshape(ROWS * FL, 128)
        im = zn[:, 1, :, lanes].reshape(ROWS * FL, 128)
        v = jnp.concatenate([re, im], axis=1)
        h_buf[g] = jnp.dot(v, tab_v[g], preferred_element_type=F32)
        return carry

    lax.fori_loop(0, NG, group, 0)

    def put(r):
        return pltpu.make_async_copy(rows_v.at[r], out_hbm.at[r], row_sem.at[r])

    def cycle(r, carry):
        rows = pl.ds(pl.multiple_of(local_row(me, r) * FL, FL), FL)
        for half in range(2):
            re = [h_buf[g, rows, pl.ds(half * 128, 128)] for g in range(NG)]
            im = [h_buf[g, rows, pl.ds(256 + half * 128, 128)] for g in range(NG)]
            c = [(re[0], None)] + [(re[g], im[g]) for g in range(1, NG)] + [(im[0], None)]
            y = idft20(c)
            for b in range(20):
                rows_v[r, :, pl.ds(b * 256 + half * 128, 128)] = y[b].astype(BF)
        put(r).start()
        return carry

    lax.fori_loop(0, ROWS, cycle, 0)

    def done(r, c):
        put(r).wait()
        return c

    lax.fori_loop(0, ROWS, done, 0)
    hand_on.wait()

ANY = pl.BlockSpec(memory_space=pl.ANY)
VM = pl.BlockSpec(memory_space=pltpu.VMEM)
SM = pl.BlockSpec(memory_space=pltpu.SMEM)
LIMIT = 56 * 2**20


def per_device(fields, depart, blend, wave_owner, damping):
    fwd_lat, bwd_lat = latitude_tables()
    dma = pltpu.SemaphoreType.DMA
    row = wave_owner.reshape(MM // 128, 128)
    r = jnp.arange(ROWS, dtype=jnp.int32)
    held = jnp.where(r < HALO, -HALO, jnp.where(r >= ROWS - HALO, ROWS - 2 * HALO, 0))
    places = (depart - ((my_index() * ROWS + held) * NB)[:, None, None]).reshape(-1)
    fourier = pl.pallas_call(
        grid_kernel,
        out_shape=jax.ShapeDtypeStruct((ROWS, 2, FL, MM), BF),
        in_specs=[ANY, SM, ANY, ANY],
        out_specs=VM,
        scratch_shapes=[
            pltpu.VMEM((ROWS, NB, FL, BW), BF),
            pltpu.VMEM((3 * HALO, NB, FL, BW), BF),
            pltpu.VMEM((3 * HALO, NB, FL, BW), BF),
            pltpu.VMEM((ROWS, NB, K, BW), F32),
            pltpu.VMEM((NG, 512, 256), BF),
            pltpu.VMEM((20, FL, 256), F32),
            pltpu.VMEM((NG, ROWS * FL, 512), BF),
            dma((3 * NB,)), dma((2,)), dma((2,)), dma((2,)),
        ],
        compiler_params=pltpu.CompilerParams(vmem_limit_bytes=LIMIT, collective_id=0, has_side_effects=True),
        name="grid_step",
    )(fields, places, blend, jnp.asarray(forward_tables()))
    zonal, spectra = pl.pallas_call(
        lat_kernel,
        out_shape=(jax.ShapeDtypeStruct((TQ, MM // 2, 2, 128), BF), jax.ShapeDtypeStruct((OWN, FL, 2, MM), F32)),
        in_specs=[VM, VM, SM, SM, ANY, ANY],
        out_specs=(ANY, ANY),
        scratch_shapes=[
            pltpu.VMEM((3 * MM, 128), F32),
            pltpu.VMEM((OWN, FL, 2, MM), F32),
            pltpu.VMEM((MM, 128), F32),
            pltpu.VMEM((MM, 128), F32),
            pltpu.VMEM((TQ, MM // 2, 2, 128), BF),
            pltpu.VMEM((NDEV, TQ, 5, 2, 128), BF),
            pltpu.VMEM((NDEV * 50, 128), F32),
            pltpu.VMEM((2, NLAT // 2, COLS), BF),
            pltpu.VMEM((2, MM // 2, COLS), BF),
            pltpu.VMEM((NDEV, TQ, 5, 2, 128), BF),
            pltpu.VMEM((2, MM // 2, NLAT // 2), BF),
            pltpu.VMEM((2, NLAT // 2, MM // 2), BF),
            dma((2,)), dma((NDEV,)), dma((NDEV,)), dma((NDEV,)), dma((NDEV,)), dma((2,)),
        ],
        compiler_params=pltpu.CompilerParams(vmem_limit_bytes=LIMIT, collective_id=1, has_side_effects=True),
        name="latitude_step",
    )(fourier, row, wave_owner, damping, jnp.asarray(fwd_lat), jnp.asarray(bwd_lat))
    updated, spectra = pl.pallas_call(
        wave_kernel,
        out_shape=(jax.ShapeDtypeStruct((ROWS, FL, NLON), BF), jax.ShapeDtypeStruct((OWN, FL, 2, MM), F32)),
        in_specs=[VM, VM, ANY, ANY],
        out_specs=(ANY, ANY),
        scratch_shapes=[
            pltpu.VMEM((MM, 128), F32),
            pltpu.VMEM((MM, MM), BF),
            pltpu.VMEM((ROWS * 32, MM), BF),
            pltpu.VMEM((ROWS, 2, FL, MM), BF),
            pltpu.VMEM((NG, ROWS * FL, 512), F32),
            pltpu.VMEM((NG, 256, 512), BF),
            pltpu.VMEM((ROWS, FL, NLON), BF),
            pltpu.VMEM((OWN, FL, 2, MM), F32),
            dma((3,)), dma((ROWS,)),
        ],
        compiler_params=pltpu.CompilerParams(vmem_limit_bytes=LIMIT),
        name="wave_step",
    )(zonal.reshape(TQ, MM, 128), row, jnp.asarray(inverse_tables()), spectra)
    return (updated, spectra)


def solution(mesh):
    in_specs = (
        P(("band", "set"), None, None),
        P(("band", "set"), None, None),
        P(("band", "set"), None, None, None),
        P(),
        P(),
    )
    out_specs = (P(("band", "set"), None, None), P(("band", "set"), None, None, None))
    return jax.shard_map(
        per_device, mesh=mesh, in_specs=in_specs, out_specs=out_specs, check_vma=False
    )
```

```python
import functools
import math

import jax
import jax.numpy as jnp
import ml_dtypes
import numpy as np
from jax import lax
from jax.experimental import pallas as pl
from jax.experimental.pallas import tpu as pltpu
from jax.sharding import PartitionSpec as P

NLAT = 2560
NLON = 5120
MM = 1280
LEV = 8
BW = 128
K = 4
HALO = 4
FL = 16
NB = 40
ROWS = 20
NDEV = 128
OWN = 10
TQ = 5
NG = 10
COLS = 384
MESH = pl.DeviceIdType.MESH
BF = jnp.bfloat16
F32 = jnp.float32


def group_waves(g):
    m2 = np.arange(64)
    if g == 0:
        return 20 * m2, 10 + 20 * m2
    return g + 20 * m2, 20 - g + 20 * m2


@functools.lru_cache(None)
def forward_tables():
    s = math.sqrt(2.0 / NLON)
    i = np.arange(256)
    out = np.zeros((NG, 512, 256))
    for g in range(NG):
        lo, hi = group_waves(g)
        for half, m in ((0, lo), (1, hi)):
            a = 2 * np.pi * ((i[:, None] * m[None, :]) % NLON) / NLON
            c, sn = s * np.cos(a), s * np.sin(a)
            re = slice(64 * half, 64 * half + 64)
            im = slice(128 + 64 * half, 192 + 64 * half)
            if g == 0:
                rows = slice(256 * half, 256 * half + 256)
                out[g, rows, re] = c
                out[g, rows, im] = -sn
            else:
                sign = 1.0 if half == 0 else -1.0
                out[g, :256, re] = c
                out[g, :256, im] = -sn
                out[g, 256:, re] = sign * sn
                out[g, 256:, im] = sign * c
    return out.astype(ml_dtypes.bfloat16)


@functools.lru_cache(None)
def inverse_tables():
    s = math.sqrt(2.0 / NLON)
    i = np.arange(256)
    out = np.zeros((NG, 256, 512))
    for g in range(NG):
        lo, hi = group_waves(g)
        for half, m in ((0, lo), (1, hi)):
            a = 2 * np.pi * ((m[:, None] * i[None, :]) % NLON) / NLON
            w = np.where(m == 0, 0.5, 1.0)[:, None] * s
            c, sn = w * np.cos(a), w * np.sin(a)
            re = slice(64 * half, 64 * half + 64)
            im = slice(128 + 64 * half, 192 + 64 * half)
            if g == 0:
                cols = slice(256 * half, 256 * half + 256)
                out[g, re, cols] = c
                out[g, im, cols] = -sn
            else:
                sign = 1.0 if half == 0 else -1.0
                out[g, re, :256] = c
                out[g, im, :256] = -sn
                out[g, re, 256:] = sign * sn
                out[g, im, 256:] = sign * c
    return out.astype(ml_dtypes.bfloat16)


@functools.lru_cache(None)
def latitude_tables():
    c, t, r, sl = np.meshgrid(np.arange(4), np.arange(TQ), np.arange(4), np.arange(16), indexing="ij")
    j = (20 * (4 * sl + c) + 4 * t + r).reshape(-1)
    n = np.arange(MM)
    g = np.where(n == 0, math.sqrt(1.0 / NLAT), math.sqrt(2.0 / NLAT))
    b = g[:, None] * np.cos(np.pi * ((n[:, None] * (2 * j[None, :] + 1)) % (4 * NLAT)) / (2 * NLAT))
    be, bo = b[0::2], b[1::2]
    fwd = np.stack([be, bo]).astype(ml_dtypes.bfloat16)
    bwd = np.stack([be.T, bo.T]).astype(ml_dtypes.bfloat16)
    return np.ascontiguousarray(fwd), np.ascontiguousarray(bwd)


C1, C2 = math.cos(2 * math.pi / 5), math.cos(4 * math.pi / 5)
S1, S2 = math.sin(2 * math.pi / 5), math.sin(4 * math.pi / 5)


def five_parts(x):
    e1, e2 = x[1] + x[4], x[2] + x[3]
    o1, o2 = x[1] - x[4], x[2] - x[3]
    total = x[0] + (e1 + e2)
    return total, x[0] + C1 * e1 + C2 * e2, x[0] + C2 * e1 + C1 * e2, S1 * o1 + S2 * o2, S2 * o1 - S1 * o2


def dft20(d):
    alpha, beta, gr, gi = [], [], [], []
    for q in range(5):
        v = [None] * 4
        for b in (q, q + 5, q + 10, q + 15):
            v[b % 4] = d[b]
        e, o = v[0] + v[2], v[1] + v[3]
        alpha.append(e + o)
        beta.append(e - o)
        gr.append(v[0] - v[2])
        gi.append(v[3] - v[1])
    out = [None] * 11
    s, e1, e2, o1, o2 = five_parts(alpha)
    out[0], out[4], out[8] = (s, None), (e1, -o1), (e2, -o2)
    s, e1, e2, o1, o2 = five_parts(beta)
    out[10], out[6], out[2] = (s, None), (e1, o1), (e2, o2)
    s, e1, e2, o1, o2 = five_parts(gr)
    t, f1, f2, p1, p2 = five_parts(gi)
    out[5] = (s, t)
    out[9] = (e1 + p1, f1 - o1)
    out[1] = (e1 - p1, f1 + o1)
    out[7] = (e2 + p2, o2 - f2)
    out[3] = (e2 - p2, -(f2 + o2))
    return out


def idft20(c):
    a, bb, dr, di = [], [], [], []

    def spread(x0, pr, mi):
        ev1 = x0 + C1 * pr[0] + C2 * pr[1]
        ev2 = x0 + C2 * pr[0] + C1 * pr[1]
        od1 = S1 * mi[0] + S2 * mi[1]
        od2 = S2 * mi[0] - S1 * mi[1]
        return [x0 + (pr[0] + pr[1]), ev1 + od1, ev2 + od2, ev2 - od2, ev1 - od1]

    a = spread(c[0][0], (c[4][0], c[8][0]), (-c[4][1], -c[8][1]))
    bb = spread(c[10][0], (c[6][0], c[2][0]), (c[6][1], c[2][1]))
    dr = spread(
        c[5][0],
        (c[1][0] + c[9][0], c[3][0] + c[7][0]),
        (c[1][1] - c[9][1], c[7][1] - c[3][1]),
    )
    di = spread(
        c[5][1],
        (c[1][1] + c[9][1], -(c[3][1] + c[7][1])),
        (c[9][0] - c[1][0], c[7][0] - c[3][0]),
    )
    plus = [a[q] + bb[q] for q in range(5)]
    minus = [a[q] - bb[q] for q in range(5)]
    out = []
    for b in range(20):
        q = b % 5
        base = plus[q] if b % 2 == 0 else minus[q]
        r = b % 4
        out.append(base + dr[q] if r == 0 else base - di[q] if r == 1 else base - dr[q] if r == 2 else base + di[q])
    return out


def my_index():
    return lax.axis_index("band") * 32 + lax.axis_index("set")


def local_row(me, p):
    return jnp.where(me < NDEV // 2, p, ROWS - 1 - p)


def place_of(d):
    far = d // (NDEV // 2)
    s = d + far * (NDEV - 1 - 2 * d)
    return far * 64 + (s % 4) * 16 + s // 4


def nat_columns(wave_ref, out_ref):
    w = wave_ref[...]
    m2 = w // 20
    m1 = w - 20 * m2
    grp = jnp.where(m1 > 10, 20 - m1, jnp.where(m1 == 10, 0, m1))
    nat = (grp * 128 + jnp.where(m1 >= 10, 64, 0) + m2).astype(F32)
    for i in range(MM // 128):
        out_ref[pl.ds(i * 128, 128), :] = jnp.transpose(
            jnp.broadcast_to(nat[i:i + 1, :], (128, 128)))


def one_hot(nat, first, count):
    lanes = first + lax.broadcasted_iota(jnp.int32, nat.shape, 1).astype(F32)
    return jnp.concatenate(
        [jnp.where(nat == lanes + 128.0 * j, 1.0, 0.0).astype(BF) for j in range(count // 128)], axis=1)


def device_of(index):
    return index // 32, index % 32


def grid_kernel(fields_ref, dep_ref, blend_hbm, tab_hbm, out_ref,
                mid, top, low, blend_v, tab_v, dep_f, g_buf, sem, big_sem, send_sem, recv_sem):
    me = my_index()
    right, left = (me + 1) % NDEV, (me + NDEV - 1) % NDEV
    barrier = pltpu.get_barrier_semaphore()
    for d in (left, right):
        pl.semaphore_signal(barrier, inc=1, device_id=device_of(d), device_id_type=MESH)
    parts = []
    for part, (first, count, ref, at) in enumerate(((0, 2 * HALO, top, HALO), (ROWS - 2 * HALO, 2 * HALO, low, 0), (0, ROWS, mid, 0))):
        parts.append([pltpu.make_async_copy(
            fields_ref.at[pl.ds(first, count), :, pl.ds(b * BW, BW)],
            ref.at[pl.ds(at, count), b], sem.at[part * NB + b]) for b in range(NB)])
    for c in parts[0] + parts[1]:
        c.start()
    load_blend = pltpu.make_async_copy(blend_hbm, blend_v, big_sem.at[0])
    load_blend.start()
    for c in parts[2]:
        c.start()
    load_tab = pltpu.make_async_copy(tab_hbm, tab_v, big_sem.at[1])
    load_tab.start()
    for c in parts[0] + parts[1]:
        c.wait()
    pl.semaphore_wait(barrier, 2)
    halos = []
    for i, (src, dst, d) in enumerate(((low.at[pl.ds(HALO, HALO)], top.at[pl.ds(0, HALO)], right),
                                       (top.at[pl.ds(HALO, HALO)], low.at[pl.ds(2 * HALO, HALO)], left))):
        halos.append(pltpu.make_async_remote_copy(
            src_ref=src, dst_ref=dst, send_sem=send_sem.at[i], recv_sem=recv_sem.at[i],
            device_id=device_of(d), device_id_type=MESH))
    for c in halos:
        c.start()
    load_blend.wait()
    for c in parts[2]:
        c.wait()

    def cycles(first, count, ref):
        blocks = ref.reshape(ref.shape[0] * NB, FL, BW)

        def cycle(r, carry):
            p = local_row(me, r)
            for b in range(NB):
                total = None
                for k in range(K):
                    at = dep_ref[(r * NB + b) * K + k]
                    term = blend_v[r, b, pl.ds(k, 1), :] * blocks[at].astype(F32)
                    total = term if total is None else total + term
                dep_f[b // 2, :, pl.ds((b % 2) * BW, BW)] = total
            rows = pl.ds(pl.multiple_of(p * FL, FL), FL)
            for half in range(2):
                lanes = pl.ds(half * 128, 128)
                g = dft20([dep_f[b, :, lanes] for b in range(20)])
                pairs = [(g[0][0], g[10][0])] + [g[i] for i in range(1, 10)]
                for i, (re, im) in enumerate(pairs):
                    g_buf[i, rows, pl.ds(half * 128, 128)] = re.astype(BF)
                    g_buf[i, rows, pl.ds(256 + half * 128, 128)] = im.astype(BF)
            return carry

        lax.fori_loop(first, first + count, cycle, 0)

    def groups(spans):
        def group(g, carry):
            lanes = pl.ds(pl.multiple_of(g * 128, 128), 128)
            u = jnp.concatenate([g_buf[g, pl.ds(first * FL, count * FL), :] for first, count in spans], axis=0)
            v = jnp.dot(u, tab_v[g], preferred_element_type=F32).astype(BF)
            at = 0
            for first, count in spans:
                rows = v[at * FL:(at + count) * FL]
                out_ref[pl.ds(first, count), 0, :, lanes] = rows[:, :128].reshape(count, FL, 128)
                out_ref[pl.ds(first, count), 1, :, lanes] = rows[:, 128:].reshape(count, FL, 128)
                at += count
            return carry

        lax.fori_loop(0, NG, group, 0)

    cycles(HALO, ROWS - 2 * HALO, mid)
    load_tab.wait()
    groups(((HALO, ROWS - 2 * HALO),))
    for c in halos:
        c.wait()
    cycles(0, HALO, top)
    cycles(ROWS - HALO, HALO, low)
    groups(((0, HALO), (ROWS - HALO, HALO)))


def block_swap(x):
    lane = lax.broadcasted_iota(jnp.int32, x[0].shape, 1)
    low64 = lane < 64
    low32 = (lane % 64) < 32
    z = [None] * 4
    for a in range(2):
        lo, hi = x[a], x[a + 2]
        z[a] = jnp.where(low64, lo, pltpu.roll(hi, 64, 1))
        z[a + 2] = jnp.where(low64, pltpu.roll(lo, 64, 1), hi)
    y = [None] * 4
    for a in (0, 2):
        lo, hi = z[a], z[a + 1]
        y[a] = jnp.where(low32, lo, pltpu.roll(hi, 32, 1))
        y[a + 1] = jnp.where(low32, pltpu.roll(lo, 96, 1), hi)
    return y


def partner(i):
    x = lax.axis_index("band")
    st = lax.axis_index("set")
    q, u = i // 32, (i * 11) % 32
    tx = (x + u // 8) % 4
    ty = (st // 8 + (u // 2) % 4) % 4
    tz = ((st // 2) % 4 + 2 * (u % 2) + q % 2) % 4
    tc = (st % 2 + (q + 1) // 2) % 2
    return tx, (ty * 4 + tz) * 2 + tc


def lat_kernel(f_ref, wave_v, wave_s, damp_s, fwd_hbm, bwd_hbm, out_ref, spec_hbm,
               st_ref, spec_v, natc, natq, xs, rx, xf, uv, s16, zs, fwd_v, bwd_v, big_sem,
               send1, recv1, send2, recv2, own_sem):
    me = my_index()
    load_fwd = pltpu.make_async_copy(fwd_hbm, fwd_v, big_sem.at[0])
    load_bwd = pltpu.make_async_copy(bwd_hbm, bwd_v, big_sem.at[1])
    load_fwd.start()
    load_bwd.start()
    barrier = pltpu.get_barrier_semaphore()
    nat_columns(wave_v, natc)

    for j in range(1, NDEV):
        pl.semaphore_signal(barrier, inc=1, device_id=partner(j), device_id_type=MESH)
    for q in range(4):
        for m in range(OWN):
            natq[pl.ds(q * 320 + m, 32, stride=OWN), :] = natc[pl.ds(q * OWN + m, 32, stride=4 * OWN), :]
    fourier = f_ref[...].reshape(ROWS * 32, MM)

    def place_sent(d):
        return pl.ds(((d % 4) * 32 + d // 4) * 5, 5)

    def to_owner(i):
        tx, ts = partner(i)
        return pltpu.make_async_remote_copy(
            src_ref=xs.at[:, place_sent(tx * 32 + ts)], dst_ref=rx.at[place_of(me)],
            send_sem=send1.at[i], recv_sem=recv1.at[i], device_id=(tx, ts), device_id_type=MESH)

    def arrived(i, c):
        to_owner(i).wait_recv()
        return c

    def left(i, c):
        to_owner(i).wait_send()
        return c

    own = pltpu.make_async_copy(xs.at[:, place_sent(me)], rx.at[place_of(me)], own_sem.at[0])
    low2 = me % 4
    flip = low2 + 1 - 2 * (low2 % 2)
    for q, bits in enumerate((low2, 3 - low2, flip, 3 - flip)):
        v = lax.dot_general(one_hot(natq[pl.ds(pl.multiple_of(bits * 320, 64), 320), :], 0.0, MM), fourier,
                            (((1,), (1,)), ((), ())), preferred_element_type=F32).astype(BF)
        for t in range(TQ):
            xs[t, pl.ds(bits * 160, 160)] = v[:, t * 128:(t + 1) * 128].reshape(160, 2, 128)
        if q == 0:
            pl.semaphore_wait(barrier, NDEV - 1)
            own.start()
        for i in range(max(1, 32 * q), 32 * q + 32):
            to_owner(i).start()
    own.wait()

    def widen(sc):
        for half in range(2):
            first = half * 64 + sc * 16
            xf[pl.ds(pl.multiple_of(first * 50, 8), 800), :] = rx[pl.ds(first, 16)].reshape(800, 128).astype(F32)

    def fold(sc, t):
        for g in range(3):
            us, vs = [], []
            for m in range(4 * g, 4 * g + 4):
                if m >= OWN:
                    us.append(jnp.zeros((16, 128), F32))
                    vs.append(jnp.zeros((16, 128), F32))
                    continue
                lo = xf[pl.ds(sc * 16 * 50 + t * OWN + m, 16, stride=50), :]
                hi = xf[pl.ds((64 + sc * 16) * 50 + t * OWN + m, 16, stride=50), :]
                us.append(lo + hi)
                vs.append(lo - hi)
            for par, vals in ((0, us), (1, vs)):
                y = block_swap(vals)
                for r in range(4):
                    rows = pl.ds(pl.multiple_of((sc * TQ + t) * 64 + r * 16, 16), 16)
                    uv[par, rows, pl.ds(g * 128, 128)] = y[r].astype(BF)

    same = ((me // 2) + me) % 2
    for stage in range(2):
        lax.fori_loop(max(1, 64 * stage), 64 * stage + 64, arrived, 0)
        low = (same + stage) % 2

        def chunk(q, carry):
            sc = low + (q // TQ) * (3 - 2 * low)

            @pl.when(q % TQ == 0)
            def _():
                widen(sc)

            fold(sc, q % TQ)
            return carry

        lax.fori_loop(0, 2 * TQ, chunk, 0)

    lane = lax.broadcasted_iota(jnp.int32, (1, COLS), 1)
    squared = (lane % FL) < LEV
    damp_row = jnp.zeros((1, COLS), F32)
    for f in range(FL):
        damp_row = jnp.where(lane % FL == f, damp_s[f], damp_row)
    wave_row = jnp.full((1, COLS), MM, jnp.int32)
    for m in range(OWN):
        wave_row = jnp.where(lane // 32 == m, wave_s[me * OWN + m], wave_row)
    load_fwd.wait()

    def analyse(i, carry):
        rows = pl.ds(pl.multiple_of(i * 128, 128), 128)
        for par in range(2):
            v = jnp.dot(fwd_v[par, rows, :], uv[par], preferred_element_type=F32)
            n = 2 * (i * 128 + lax.broadcasted_iota(jnp.int32, (128, COLS), 0)) + par
            nf = n.astype(F32)
            q = nf * (nf + 1.0) * (1.0 / (MM * (MM - 1.0)))
            qp = jnp.where(squared, q * q, q)
            v = v * (1.0 / (1.0 + damp_row * qp))
            v = jnp.where(n >= wave_row, v, 0.0)
            for g in range(3):
                st_ref[pl.ds(g * MM + i * 256 + par, 128, stride=2), :] = v[:, g * 128:(g + 1) * 128]
            s16[par, rows, :] = v.astype(BF)
        return carry

    lax.fori_loop(0, 5, analyse, 0)
    load_bwd.wait()
    turn = me % 4

    my_x, my_y, my_z = me // 32, (me // 8) % 4, (me // 4) % 2

    def to_cycles(place, d):
        return pltpu.make_async_remote_copy(
            src_ref=zs.at[place], dst_ref=out_ref.at[:, pl.ds(me * 5, 5)],
            send_sem=send2.at[place], recv_sem=recv2.at[me], device_id=device_of(d), device_id_type=MESH)

    keep = pltpu.make_async_copy(zs.at[place_of(me)], out_ref.at[:, pl.ds(me * 5, 5)], own_sem.at[1])

    def synth(i, carry):
        c = (i + turn) % 4
        rows = pl.ds(pl.multiple_of(c * 320, 320), 320)
        p = jnp.dot(bwd_v[0, rows, :], s16[0], preferred_element_type=F32)
        q = jnp.dot(bwd_v[1, rows, :], s16[1], preferred_element_type=F32)
        for half, z in ((0, p + q), (1, p - q)):
            first = (half * 64 + c * 16) * 50
            for t in range(TQ):
                for g in range(3):
                    y = block_swap([z[(t * 4 + r) * 16:(t * 4 + r + 1) * 16, g * 128:(g + 1) * 128] for r in range(4)])
                    for m in range(4 * g, min(4 * g + 4, OWN)):
                        xf[pl.ds(first + t * OWN + m, 16, stride=50), :] = y[m - 4 * g]
            zs[pl.ds(half * 64 + c * 16, 16)] = (
                xf[pl.ds(pl.multiple_of(first, 8), 800), :].astype(BF).reshape(16, TQ, 5, 2, 128))

        for j in range(32):
            k = (j * 11) % 32
            tx, ty, tz = (my_x + k // 8) % 4, (my_y + (k // 2) % 4) % 4, (my_z + k % 2) % 2
            far = tx // 2
            low_bits = c + far * (3 - 2 * c)
            d = tx * 32 + ty * 8 + tz * 4 + low_bits
            place = far * 64 + c * 16 + (d // 4 + far * (31 - 2 * (d // 4)))
            if k > 0:
                to_cycles(place, d).start()
                continue

            @pl.when(d != me)
            def _():
                to_cycles(place, d).start()

            @pl.when(d == me)
            def _():
                keep.start()

        return carry

    lax.fori_loop(0, 4, synth, 0)
    for g in range(3):
        for nt in range(10):
            tr = jnp.transpose(st_ref[pl.ds(g * MM + nt * 128, 128), :])
            for m in range(4 * g, min(4 * g + 4, OWN)):
                for c in range(2):
                    first = (m - 4 * g) * 32 + c * 16
                    spec_v[m, :, c, pl.ds(nt * 128, 128)] = tr[first:first + 16]
    put_spec = pltpu.make_async_copy(spec_v, spec_hbm, big_sem.at[0])
    put_spec.start()
    keep.wait()
    lax.fori_loop(1, NDEV, left, 0)

    def finish(i, c):
        d = (me + i) % NDEV
        place = place_of(d)
        pltpu.make_async_remote_copy(
            src_ref=zs.at[place], dst_ref=out_ref.at[:, pl.ds(d * 5, 5)],
            send_sem=send2.at[place], recv_sem=recv2.at[d], device_id=device_of(d), device_id_type=MESH).wait()
        return c

    lax.fori_loop(1, NDEV, finish, 0)
    put_spec.wait()


def wave_kernel(x_ref, wave_v, tab_hbm, spec_in, out_hbm, spec_out,
                natc, hot, zt, zn, h_buf, tab_v, rows_v, spec_v, big_sem, row_sem):
    me = my_index()
    load_tab = pltpu.make_async_copy(tab_hbm, tab_v, big_sem.at[0])
    load_tab.start()
    take = pltpu.make_async_copy(spec_in, spec_v, big_sem.at[1])
    hand_on = pltpu.make_async_copy(spec_v, spec_out, big_sem.at[2])
    take.start()
    nat_columns(wave_v, natc)

    def hots(i, c):
        rows = pl.ds(pl.multiple_of(i * 128, 128), 128)
        hot[rows, :] = one_hot(natc[rows, :], 0.0, MM)
        return c

    lax.fori_loop(0, MM // 128, hots, 0)

    def turn(t, carry):
        zt[pl.ds(pl.multiple_of(t * 128, 128), 128), :] = jnp.transpose(x_ref[t])
        return carry

    lax.fori_loop(0, TQ, turn, 0)

    def order(i, carry):
        lanes = pl.ds(pl.multiple_of(i * 256, 256), 256)
        v = jnp.dot(zt[...], hot[:, lanes], preferred_element_type=F32).astype(BF)
        zn[:, :, :, lanes] = v.reshape(ROWS, 2, FL, 256)
        return carry

    lax.fori_loop(0, MM // 256, order, 0)
    load_tab.wait()
    take.wait()
    hand_on.start()

    def group(g, carry):
        lanes = pl.ds(pl.multiple_of(g * 128, 128), 128)
        re = zn[:, 0, :, lanes].reshape(ROWS * FL, 128)
        im = zn[:, 1, :, lanes].reshape(ROWS * FL, 128)
        v = jnp.concatenate([re, im], axis=1)
        h_buf[g] = jnp.dot(v, tab_v[g], preferred_element_type=F32)
        return carry

    lax.fori_loop(0, NG, group, 0)

    def put(r):
        return pltpu.make_async_copy(rows_v.at[r], out_hbm.at[r], row_sem.at[r])

    def cycle(r, carry):
        rows = pl.ds(pl.multiple_of(local_row(me, r) * FL, FL), FL)
        for half in range(2):
            re = [h_buf[g, rows, pl.ds(half * 128, 128)] for g in range(NG)]
            im = [h_buf[g, rows, pl.ds(256 + half * 128, 128)] for g in range(NG)]
            c = [(re[0], None)] + [(re[g], im[g]) for g in range(1, NG)] + [(im[0], None)]
            y = idft20(c)
            for b in range(20):
                rows_v[r, :, pl.ds(b * 256 + half * 128, 128)] = y[b].astype(BF)
        put(r).start()
        return carry

    lax.fori_loop(0, ROWS, cycle, 0)

    def done(r, c):
        put(r).wait()
        return c

    lax.fori_loop(0, ROWS, done, 0)
    hand_on.wait()

ANY = pl.BlockSpec(memory_space=pl.ANY)
VM = pl.BlockSpec(memory_space=pltpu.VMEM)
SM = pl.BlockSpec(memory_space=pltpu.SMEM)
LIMIT = 56 * 2**20


def per_device(fields, depart, blend, wave_owner, damping):
    fwd_lat, bwd_lat = latitude_tables()
    dma = pltpu.SemaphoreType.DMA
    row = wave_owner.reshape(MM // 128, 128)
    r = jnp.arange(ROWS, dtype=jnp.int32)
    held = jnp.where(r < HALO, -HALO, jnp.where(r >= ROWS - HALO, ROWS - 2 * HALO, 0))
    places = (depart - ((my_index() * ROWS + held) * NB)[:, None, None]).reshape(-1)
    fourier = pl.pallas_call(
        grid_kernel,
        out_shape=jax.ShapeDtypeStruct((ROWS, 2, FL, MM), BF),
        in_specs=[ANY, SM, ANY, ANY],
        out_specs=VM,
        scratch_shapes=[
            pltpu.VMEM((ROWS, NB, FL, BW), BF),
            pltpu.VMEM((3 * HALO, NB, FL, BW), BF),
            pltpu.VMEM((3 * HALO, NB, FL, BW), BF),
            pltpu.VMEM((ROWS, NB, K, BW), F32),
            pltpu.VMEM((NG, 512, 256), BF),
            pltpu.VMEM((20, FL, 256), F32),
            pltpu.VMEM((NG, ROWS * FL, 512), BF),
            dma((3 * NB,)), dma((2,)), dma((2,)), dma((2,)),
        ],
        compiler_params=pltpu.CompilerParams(vmem_limit_bytes=LIMIT, collective_id=0, has_side_effects=True),
        name="grid_step",
    )(fields, places, blend, jnp.asarray(forward_tables()))
    zonal, spectra = pl.pallas_call(
        lat_kernel,
        out_shape=(jax.ShapeDtypeStruct((TQ, MM // 2, 2, 128), BF), jax.ShapeDtypeStruct((OWN, FL, 2, MM), F32)),
        in_specs=[VM, VM, SM, SM, ANY, ANY],
        out_specs=(ANY, ANY),
        scratch_shapes=[
            pltpu.VMEM((3 * MM + 64, 128), F32),
            pltpu.VMEM((OWN, FL, 2, MM), F32),
            pltpu.VMEM((MM + 64, 128), F32),
            pltpu.VMEM((MM + 64, 128), F32),
            pltpu.VMEM((TQ, MM // 2, 2, 128), BF),
            pltpu.VMEM((NDEV, TQ, 5, 2, 128), BF),
            pltpu.VMEM((NDEV * 50 + 64, 128), F32),
            pltpu.VMEM((2, NLAT // 2, COLS), BF),
            pltpu.VMEM((2, MM // 2, COLS), BF),
            pltpu.VMEM((NDEV, TQ, 5, 2, 128), BF),
            pltpu.VMEM((2, MM // 2, NLAT // 2), BF),
            pltpu.VMEM((2, NLAT // 2, MM // 2), BF),
            dma((2,)), dma((NDEV,)), dma((NDEV,)), dma((NDEV,)), dma((NDEV,)), dma((2,)),
        ],
        compiler_params=pltpu.CompilerParams(vmem_limit_bytes=LIMIT, collective_id=1, has_side_effects=True),
        name="latitude_step",
    )(fourier, row, wave_owner, damping, jnp.asarray(fwd_lat), jnp.asarray(bwd_lat))
    updated, spectra = pl.pallas_call(
        wave_kernel,
        out_shape=(jax.ShapeDtypeStruct((ROWS, FL, NLON), BF), jax.ShapeDtypeStruct((OWN, FL, 2, MM), F32)),
        in_specs=[VM, VM, ANY, ANY],
        out_specs=(ANY, ANY),
        scratch_shapes=[
            pltpu.VMEM((MM, 128), F32),
            pltpu.VMEM((MM, MM), BF),
            pltpu.VMEM((ROWS * 32, MM), BF),
            pltpu.VMEM((ROWS, 2, FL, MM), BF),
            pltpu.VMEM((NG, ROWS * FL, 512), F32),
            pltpu.VMEM((NG, 256, 512), BF),
            pltpu.VMEM((ROWS, FL, NLON), BF),
            pltpu.VMEM((OWN, FL, 2, MM), F32),
            dma((3,)), dma((ROWS,)),
        ],
        compiler_params=pltpu.CompilerParams(vmem_limit_bytes=LIMIT),
        name="wave_step",
    )(zonal.reshape(TQ, MM, 128), row, jnp.asarray(inverse_tables()), spectra)
    return (updated, spectra)


def solution(mesh):
    in_specs = (
        P(("band", "set"), None, None),
        P(("band", "set"), None, None),
        P(("band", "set"), None, None, None),
        P(),
        P(),
    )
    out_specs = (P(("band", "set"), None, None), P(("band", "set"), None, None, None))
    return jax.shard_map(
        per_device, mesh=mesh, in_specs=in_specs, out_specs=out_specs, check_vma=False
    )
```
